32 devices in a mesh: outer: 4 (over y, core), inner: 8 (over z, x).
Axes of the slice: x: 2, y: 2, z: 4, core: 2. Of those that a mesh axis runs over, the one named last changes fastest.
Arguments:
- queries: bfloat16 [4096, 2048], P(('outer', 'inner')), may hold values from -6 to 6
- key_vectors: bfloat16 [4096, 2048], P(('outer', 'inner')), may hold values from -6 to 6
- value_vectors: bfloat16 [4096, 2048], P(('outer', 'inner')), may hold values from -6 to 6
- segment_ids: int32 [4096], P(('outer', 'inner')), may hold values from 0 to 15, never falling along the last dimension, each value on 1 to 1024 neighbouring positions
- ridge_weight: float32 [16], replicated, may hold values from 2 to 32
Outputs:
- readout: float32 [4096, 2048], P(('outer', 'inner'))
The draws below stay inside these ranges and needn't reach their ends.
Inputs may be any that keep to these rules, and one draw needn't show every extreme that they name: `segment_ids`: segment ids never fall along the sequence; each document has 1 to 1024 tokens and one has exactly 1024.
All inputs are finite; a program needn't handle non-finite values.
Results may differ from the reference program's by a relative error of at most 0.0003.
Values sent between devices are 32-bit elements; how exact they have to be, the bound alone decides.
No kernel may reach another device: no remote copies, remote signals or barrier semaphores. Data moves between devices by JAX's collectives and lax.ppermute only.
A program may use at most 128 MiB of HBM per device.

```python
import math
import jax
import jax.numpy as jnp
import numpy as np
from jax import lax

H = 16
E = 128
CG_ITERS = 3
DOCS = 16
TOKENS = 4096
DOC_MOST = 1024


def levels(own_key, shape, cuts, low, top_value):
    factor_of = 1.0
    for dim, blocks in cuts:
        steps = jax.random.uniform(jax.random.fold_in(jax.random.fold_in(own_key, 6), dim), (blocks,), jnp.float32, low / len(cuts), top_value / len(cuts))
        factor_of = factor_of * jnp.repeat(jnp.exp(steps), shape[dim] // blocks).reshape((-1,) + (1,) * (len(shape) - 1 - dim))
    return factor_of


def split_up(amount, total, most, skew):
    portions = [(1 << 20) // math.isqrt(rank ** skew) + 1 for rank in range(2, amount + 1)]
    surplus, given = total - most - (amount - 1), [1] * (amount - 1)
    while surplus > 0:
        candidates = [i for i in range(amount - 1) if given[i] < most]
        mass, left = sum([portions[i] for i in candidates]), surplus
        for i in candidates:
            addition = min(most - given[i], max(1, left * portions[i] // mass), surplus)
            given[i] = given[i] + addition
            surplus = surplus - addition
    return np.array([most] + given)


def uneven(rng, number_of, total, limit, skew):
    if number_of == 2:
        one = jax.random.randint(rng, (), max(1, total - limit), min(limit, total - 1) + 1)
        return jnp.stack([one, total - one])
    lengths = jnp.asarray(split_up(number_of, total, limit, skew), jnp.int32)
    twos = (number_of - 1) // 2
    source_of, sink = lengths[1:1 + 2 * twos:2], lengths[2:2 + 2 * twos:2]
    room = jnp.minimum(source_of - 1, limit - sink)
    shifted = jax.random.randint(jax.random.fold_in(rng, 1), (twos,), 0, 1 << 20) % (room + 1)
    lengths = lengths.at[1:1 + 2 * twos:2].set(source_of - shifted).at[2:2 + 2 * twos:2].set(sink + shifted)
    return lengths[jax.random.permutation(jax.random.fold_in(rng, 2), number_of)]


def noise(key, dims, scale, most, split=(), dtype=jnp.bfloat16):
    entries = scale * jax.random.normal(key, dims, jnp.float32)
    if split:
        entries = entries * levels(key, dims, split, -0.22, 0.18)
    return jnp.clip(entries, -most, most).astype(dtype)


def setup_inputs(seed: int = 0) -> dict:
    keys = jax.random.split(jax.random.key(seed), 6)
    queries = noise(keys[0], (TOKENS, H * E), 1.0, 6.0, ((0, 32),))
    key_vectors = noise(keys[1], (TOKENS, H * E), 1.0, 6.0, ((0, 32),))
    value_vectors = noise(keys[2], (TOKENS, H * E), 1.0, 6.0, ((0, 32),))
    segment_ids = jnp.searchsorted(jnp.cumsum(uneven(keys[3], DOCS, TOKENS, DOC_MOST, 1)), jnp.arange(TOKENS), side="right").astype(jnp.int32)
    ridge_weight = jnp.clip(jnp.exp(jax.random.uniform(keys[4], (H,), jnp.float32, math.log(2.0), math.log(32.0))), 2.0, 32.0)
    return dict(queries=queries, key_vectors=key_vectors, value_vectors=value_vectors, segment_ids=segment_ids, ridge_weight=ridge_weight)


highest = lax.Precision.HIGHEST
block_rows = 128

def normed(values_in):
    widened = values_in.astype(jnp.float32)
    return widened * lax.rsqrt(lax.optimization_barrier(jnp.sum(widened * widened, -1, keepdims=True)) + 1e-06)

def combine(earlier, latter):
    early_last, early_gram, early_cross = earlier
    late_last, late_gram, late_cross = latter
    keep_mask = jnp.logical_or(early_last == late_last, late_last < 0).astype(jnp.float32)
    return (jnp.where(late_last < 0, early_last, late_last), late_gram + keep_mask * early_gram, late_cross + keep_mask * early_cross)

def summarize(key_rows, value_rows, segment):
    last_value = segment[-1]
    weight = (segment == last_value).astype(jnp.float32)[None, :, None]
    gram = jnp.einsum('hbe,hbf->hef', key_rows * weight, key_rows, precision=highest)
    cross = jnp.einsum('hbv,hbk->hvk', value_rows * weight, key_rows, precision=highest)
    return (last_value.astype(jnp.float32), gram, cross)

def span_solve(query_rows, key_rows, value_rows, segment, prefix, ridge_weight):
    prev_last, gram_in, cross_in = prefix
    segment_value = segment.astype(jnp.float32)
    carried = (segment_value == prev_last).astype(jnp.float32)[None, :, None]
    position = jnp.arange(segment.shape[0])
    within = jnp.logical_and(position[:, None] >= position[None, :], segment[:, None] == segment[None, :]).astype(jnp.float32)[None]

    def apply_gram(search):
        from_state = jnp.einsum('hbf,hef->hbe', search, gram_in, precision=highest) * carried
        scores = jnp.einsum('hte,hse->hts', search, key_rows, precision=highest) * within
        local_part = jnp.einsum('hts,hse->hte', scores, key_rows, precision=highest)
        return from_state + local_part + ridge_weight[:, None, None] * search
    solved = jnp.zeros_like(query_rows)
    remain = query_rows
    search = query_rows
    remain_square = lax.optimization_barrier(jnp.sum(remain * remain, -1, keepdims=True))
    for _ in range(CG_ITERS):
        applied = apply_gram(search)
        stepsize = remain_square / lax.optimization_barrier(jnp.sum(search * applied, -1, keepdims=True))
        solved = solved + stepsize * search
        remain = remain - stepsize * applied
        next_square = lax.optimization_barrier(jnp.sum(remain * remain, -1, keepdims=True))
        search = remain + next_square / remain_square * search
        remain_square = next_square
    from_state = jnp.einsum('hbk,hvk->hbv', solved, cross_in, precision=highest) * carried
    scores = jnp.einsum('hte,hse->hts', solved, key_rows, precision=highest) * within
    return from_state + jnp.einsum('hts,hsv->htv', scores, value_rows, precision=highest)

def reference(queries, key_vectors, value_vectors, segment_ids, ridge_weight):
    head_count = ridge_weight.shape[0]
    head_width = queries.shape[1] // head_count
    block_count = queries.shape[0] // block_rows

    def blocks(values_in):
        return values_in.reshape(block_count, block_rows, head_count, head_width)

    def advance(carried_state, inputs):
        query_block, key_block, value_block, segment = inputs
        query_rows = normed(query_block).transpose(1, 0, 2)
        key_rows = normed(key_block).transpose(1, 0, 2)
        value_rows = value_block.astype(jnp.float32).transpose(1, 0, 2)
        result = span_solve(query_rows, key_rows, value_rows, segment, carried_state, ridge_weight)
        updated = combine(carried_state, summarize(key_rows, value_rows, segment))
        return (updated, result.transpose(1, 0, 2))
    zeros_state = jnp.zeros((head_count, head_width, head_width), jnp.float32)
    start = (jnp.float32(-1.0), zeros_state, zeros_state)
    _, results = lax.scan(advance, start, (blocks(queries), blocks(key_vectors), blocks(value_vectors), segment_ids.reshape(block_count, block_rows)))
    return results.reshape(queries.shape[0], head_count * head_width)
```

```python
import functools

import jax
import jax.numpy as jnp
from jax import lax
from jax.experimental import pallas as pl
from jax.experimental.pallas import tpu as pltpu
from jax.sharding import Mesh
from jax.sharding import PartitionSpec as P

CG_ITERS = 3
DOC_SHARE = 4
EXTRA = 8


def split(x):
    high = x.astype(jnp.bfloat16)
    low = (x - high.astype(jnp.float32)).astype(jnp.bfloat16)
    return high, low


def dot(a, b):
    return lax.dot_general(a, b, (((1,), (0,)), ((), ())), preferred_element_type=jnp.float32)


def dot_rows(a, b):
    return lax.dot_general(a, b, (((0,), (0,)), ((), ())), preferred_element_type=jnp.float32)


def grid_ids(width):
    row = lax.broadcasted_iota(jnp.int32, (width, width), 0)
    col = lax.broadcasted_iota(jnp.int32, (width, width), 1)
    return row, col


def own_kernel(base, width, pairs, me_ref, k_ref, v_ref, weight_ref, ids_ref, *outs):
    row, col = grid_ids(width)
    upper, diagonal = row <= col, row == col
    weight = weight_ref[...]
    for slot, out in enumerate(outs):
        part = me_ref[0] ^ slot
        for pair in range(pairs):
            top = pair * (3 * width + EXTRA)
            grams = []
            for side in range(2):
                head = base + (part * pairs + pair) * 2 + side
                lanes = pl.ds(pl.multiple_of(head * width, width), width)
                keys = k_ref[:, lanes]
                wide = keys.astype(jnp.float32)
                scale = lax.rsqrt(jnp.sum(wide * wide, -1, keepdims=True) + 1e-06)
                light = weight * scale
                k_high, k_low = split(light * scale * wide)
                v_high, v_low = split(light * v_ref[:, lanes].astype(jnp.float32))
                right = jnp.concatenate(
                    [jnp.concatenate([k_high, v_high], 1), jnp.concatenate([k_low, v_low], 1)], 0
                )
                both = dot_rows(jnp.concatenate([keys, keys], 0), right)
                grams.append(both[:, :width])
                out[pl.ds(top + (1 + side) * width, width), :] = both[:, width:]
            out[pl.ds(top, width), :] = jnp.where(upper, grams[0], grams[1])
            second = jnp.sum(jnp.where(diagonal, grams[1], 0.0), 0, keepdims=True)
            out[pl.ds(top + 3 * width, EXTRA), :] = jnp.concatenate(
                [second, ids_ref[...], jnp.zeros((EXTRA - 3, width), jnp.float32)], 0
            )


def total_kernel(width, pairs, *refs):
    slots, out = refs[:-1], refs[-1]
    first_row = 3 * width + 1
    last = [slot[pl.ds(first_row + 1, 1), :] for slot in slots]
    newest = functools.reduce(jnp.maximum, last)
    keep = [(one == newest).astype(jnp.float32) for one in last]
    out[...] = functools.reduce(lambda a, b: a + b, [slot[...] * k for slot, k in zip(slots, keep)])
    for pair in range(pairs):
        out[pl.ds(pair * (3 * width + EXTRA) + first_row, 2), :] = jnp.concatenate([newest, newest], 0)


def prefix_kernel(width, slot_count, me_ref, *refs):
    slots, carries, outs = refs[:slot_count], refs[slot_count:-slot_count], refs[-slot_count:]
    first_row = 3 * width + 1
    first = [slot[pl.ds(first_row, 1), :] for slot in slots]
    last = [slot[pl.ds(first_row + 1, 1), :] for slot in slots]
    oldest = functools.reduce(jnp.minimum, first)
    carry = None
    for one in carries:
        term = one[...] * (one[pl.ds(first_row + 1, 1), :] == oldest).astype(jnp.float32)
        carry = term if carry is None else carry + term
    me = me_ref[0]
    for target, out in enumerate(outs):
        total = carry * (first[target] == oldest).astype(jnp.float32)
        for source in range(slot_count):
            if source != target:
                before = jnp.where((me ^ source) < (me ^ target), 1.0, 0.0)
                total = total + slots[source][...] * ((last[source] == first[target]).astype(jnp.float32) * before)
        out[...] = total


def solve_heads(heads, within, carried):
    prepared = []
    for queries, keys, values, gram, cross, ridge in heads:
        wide = queries.astype(jnp.float32)
        query = wide * lax.rsqrt(jnp.sum(wide * wide, -1, keepdims=True) + 1e-06)
        turned = keys.astype(jnp.float32).T
        scale = lax.rsqrt(jnp.sum(turned * turned, 0, keepdims=True) + 1e-06)
        turned = turned.astype(jnp.bfloat16)
        g_high, g_low = split(gram)
        c_high, c_low = split(cross)
        state = jnp.concatenate([g_high, turned], 1)
        final = jnp.concatenate([c_high, turned], 1)
        prepared.append(
            dict(
                state=jnp.concatenate([state, state], 0),
                state_low=g_low,
                final=jnp.concatenate([final, final], 0),
                final_low=c_low,
                keys=jnp.concatenate([keys, keys], 0),
                values=jnp.concatenate([values, values], 0),
                once=within * scale,
                twice=within * (scale * scale),
                ridge=ridge,
                solved=None,
                remain=query,
                search=query,
                square=jnp.sum(query * query, -1, keepdims=True),
            )
        )
    width = heads[0][3].shape[0]

    def product(vector, both, low, mask, rows):
        high_part, low_part = split(vector)
        wide = dot(jnp.concatenate([high_part, low_part], 1), both)
        from_state = (wide[:, :width] + dot(high_part, low)) * carried
        high_score, low_score = split(wide[:, width:] * mask)
        return from_state + dot(jnp.concatenate([high_score, low_score], 1), rows)

    for step in range(CG_ITERS):
        for h in prepared:
            search = h["search"]
            applied = product(search, h["state"], h["state_low"], h["twice"], h["keys"]) + h["ridge"] * search
            size = h["square"] / jnp.sum(search * applied, -1, keepdims=True)
            h["solved"] = size * search if step == 0 else h["solved"] + size * search
            if step < CG_ITERS - 1:
                remain = h["remain"] - size * applied
                square = jnp.sum(remain * remain, -1, keepdims=True)
                h["search"] = remain + square / h["square"] * search
                h["remain"], h["square"] = remain, square
    return [product(h["solved"], h["final"], h["final_low"], h["once"], h["values"]) for h in prepared]


def solve_kernel(base, width, pairs, slot_count, me_ref, ridge_ref, q_ref, k_ref, v_ref, within_ref, carried_ref, *refs):
    slots, out = refs[:slot_count], refs[-1]
    row, col = grid_ids(width)
    upper, diagonal = row <= col, row == col
    within, carried = within_ref[...], carried_ref[...]
    for slot, state in enumerate(slots):
        part = me_ref[0] ^ slot
        for pair in range(pairs):
            top = pair * (3 * width + EXTRA)
            packed = state[pl.ds(top, width), :]
            turned = packed.T
            second = state[pl.ds(top + 3 * width, 1), :]
            grams = [
                jnp.where(upper, packed, turned),
                jnp.where(diagonal, second, jnp.where(upper, turned, packed)),
            ]
            heads = []
            for side in range(2):
                local = (part * pairs + pair) * 2 + side
                lanes = pl.ds(pl.multiple_of((base + local) * width, width), width)
                cross = state[pl.ds(top + (1 + side) * width, width), :]
                heads.append((q_ref[:, lanes], k_ref[:, lanes], v_ref[:, lanes], grams[side], cross, ridge_ref[base + local]))
            for side, result in enumerate(solve_heads(heads, within, carried)):
                local = (part * pairs + pair) * 2 + side
                out[:, pl.ds(pl.multiple_of(local * width, width), width)] = result


VMEM = pl.BlockSpec(memory_space=pltpu.VMEM)
SMEM = pl.BlockSpec(memory_space=pltpu.SMEM)
PARAMS = pltpu.CompilerParams(vmem_limit_bytes=48 * 1024 * 1024)


def on_device(queries, key_vectors, value_vectors, segment_ids, ridge_weight, *, pieces):
    row_count, columns = queries.shape
    head_count = ridge_weight.shape[0]
    width = columns // head_count
    outer, half, near = lax.axis_size("outer"), lax.axis_size("half"), lax.axis_size("near")
    blocks = outer * half
    pairs = head_count // (2 * pieces * near)
    rows = pairs * (3 * width + EXTRA)
    back = -(-(row_count * near * blocks // DOC_SHARE - 1) // (row_count * near))

    me = lax.axis_index("near").astype(jnp.int32).reshape(1)
    segment = segment_ids.astype(jnp.float32)
    weight = (segment == segment[-1]).astype(jnp.float32)[:, None]
    carried = (segment == segment[0]).astype(jnp.float32)[:, None]
    ids = jnp.broadcast_to(jnp.stack([segment[0], segment[-1]])[:, None] + 1.0, (2, width))
    position = jnp.arange(row_count)
    within = jnp.logical_and(
        position[:, None] >= position[None, :], segment[:, None] == segment[None, :]
    ).astype(jnp.float32)

    def exchange(slots):
        return [slots[0]] + [
            lax.ppermute(slots[j], "near", [(i, i ^ j) for i in range(near)]) for j in range(1, near)
        ]

    shape = jax.ShapeDtypeStruct((rows, width), jnp.float32)
    prefixes = []
    for piece in range(pieces):
        base = piece * pairs * near * 2
        own = pl.pallas_call(
            functools.partial(own_kernel, base, width, pairs),
            out_shape=[shape] * near,
            in_specs=[SMEM, VMEM, VMEM, VMEM, VMEM],
            out_specs=[VMEM] * near,
            compiler_params=PARAMS,
            name="own_sums",
        )(me, key_vectors, value_vectors, weight, ids)
        slots = exchange(own)
        total = pl.pallas_call(
            functools.partial(total_kernel, width, pairs),
            out_shape=shape,
            in_specs=[VMEM] * near,
            out_specs=VMEM,
            compiler_params=PARAMS,
            name="block_total",
        )(*slots)
        carries = [
            lax.ppermute(total, ("outer", "half"), [(i, i + step) for i in range(blocks - step)])
            for step in range(1, min(back, blocks - 1) + 1)
        ]
        prefix = pl.pallas_call(
            functools.partial(prefix_kernel, width, near),
            out_shape=[shape] * near,
            in_specs=[SMEM] + [VMEM] * (near + len(carries)),
            out_specs=[VMEM] * near,
            compiler_params=PARAMS,
            name="prefixes",
        )(me, *slots, *carries)
        prefixes.append(exchange(prefix))
    out = None
    for piece in range(pieces):
        base = piece * pairs * near * 2
        span = pairs * near * 2 * width
        arguments = [me, ridge_weight, queries, key_vectors, value_vectors, within, carried, *prefixes[piece]]
        in_specs = [SMEM, SMEM, VMEM, VMEM, VMEM, VMEM, VMEM] + [VMEM] * near
        aliases = {}
        if out is not None:
            aliases = {len(arguments): 0}
            arguments.append(out)
            in_specs.append(pl.BlockSpec(memory_space=pl.ANY))
        out = pl.pallas_call(
            functools.partial(solve_kernel, base, width, pairs, near),
            grid=(1,),
            out_shape=jax.ShapeDtypeStruct((row_count, columns), jnp.float32),
            in_specs=in_specs,
            out_specs=pl.BlockSpec((row_count, span), functools.partial(lambda p, i: (0, p), piece)),
            input_output_aliases=aliases,
            compiler_params=PARAMS,
            name="solve",
        )(*arguments)
    return out


def solution(mesh):
    outer, inner = mesh.shape["outer"], mesh.shape["inner"]
    near = inner // 2
    finer = Mesh(mesh.devices.reshape(outer, 2, near), ("outer", "half", "near"))
    tokens = ("outer", "half", "near")

    def run(queries, key_vectors, value_vectors, segment_ids, ridge_weight):
        pieces = max(1, min(2, ridge_weight.shape[0] // (2 * near)))
        return jax.shard_map(
            functools.partial(on_device, pieces=pieces),
            mesh=finer,
            in_specs=(P(tokens, None), P(tokens, None), P(tokens, None), P(tokens), P()),
            out_specs=P(tokens, None),
            check_vma=False,
        )(queries, key_vectors, value_vectors, segment_ids, ridge_weight)

    return run
```

```python
import functools

import jax
import jax.numpy as jnp
from jax import lax
from jax.experimental import pallas as pl
from jax.experimental.pallas import tpu as pltpu
from jax.sharding import Mesh
from jax.sharding import PartitionSpec as P

CG_ITERS = 3
DOC_SHARE = 4
EXTRA = 8


def split(x):
    high = x.astype(jnp.bfloat16)
    low = (x - high.astype(jnp.float32)).astype(jnp.bfloat16)
    return high, low


def dot(a, b):
    return lax.dot_general(a, b, (((1,), (0,)), ((), ())), preferred_element_type=jnp.float32)


def dot_rows(a, b):
    return lax.dot_general(a, b, (((0,), (0,)), ((), ())), preferred_element_type=jnp.float32)


def total(terms):
    return functools.reduce(lambda a, b: a + b, terms)


def triangle(width):
    row = lax.broadcasted_iota(jnp.int32, (width, width), 0)
    col = lax.broadcasted_iota(jnp.int32, (width, width), 1)
    return row <= col, row == col


def down(ids):
    count = ids.shape[1]
    return jnp.broadcast_to(ids, (count, count)).T[:, :1]


def last_weight(ids_ref, width):
    ids = ids_ref[...].astype(jnp.float32)
    newest = jnp.max(ids, 1, keepdims=True)
    weight = (down(ids) == newest).astype(jnp.float32)
    return ids, newest, jnp.broadcast_to(weight, (ids.shape[1], width))


def row_scale(wide):
    return lax.rsqrt(jnp.sum(wide * wide, -1, keepdims=True) + 1e-06)


def own_gram_kernel(width, pairs, me_ref, ids_ref, k_hbm, *refs):
    outs, (k_ref, sems) = refs[:-2], refs[-2:]
    span = pairs * 2 * width
    copies = []
    for slot in range(len(outs)):
        start = pl.multiple_of((me_ref[0] ^ slot) * span, span)
        copy = pltpu.make_async_copy(k_hbm.at[:, pl.ds(start, span)], k_ref.at[slot], sems.at[slot])
        copy.start()
        copies.append(copy)
    upper, diagonal = triangle(width)
    ids, newest, weight = last_weight(ids_ref, width)
    oldest = jnp.min(ids, 1, keepdims=True)
    marks = [jnp.broadcast_to(one + 1.0, (1, width)) for one in (oldest, newest)]
    filler = jnp.zeros((EXTRA - 3, width), jnp.float32)
    for slot, out in enumerate(outs):
        copies[slot].wait()
        for pair in range(pairs):
            grams = []
            for side in range(2):
                keys = k_ref[slot, :, pl.ds((pair * 2 + side) * width, width)]
                wide = keys.astype(jnp.float32)
                scale = row_scale(wide)
                high, low = split(weight * (scale * scale) * wide)
                grams.append(dot_rows(jnp.concatenate([keys, keys], 0), jnp.concatenate([high, low], 0)))
            top = pair * (width + EXTRA)
            out[pl.ds(top, width), :] = jnp.where(upper, grams[0], grams[1])
            second = jnp.sum(jnp.where(diagonal, grams[1], 0.0), 0, keepdims=True)
            out[pl.ds(top + width, EXTRA), :] = jnp.concatenate([second, *marks, filler], 0)


def own_cross_kernel(width, heads, me_ref, ids_ref, k_ref, v_ref, *outs):
    weight = last_weight(ids_ref, width)[2]
    for slot, out in enumerate(outs):
        for head in range(heads):
            lanes = pl.ds(pl.multiple_of(((me_ref[0] ^ slot) * heads + head) * width, width), width)
            keys = k_ref[:, lanes]
            scale = row_scale(keys.astype(jnp.float32))
            high, low = split(weight * scale * v_ref[:, lanes].astype(jnp.float32))
            out[pl.ds(head * width, width), :] = dot_rows(
                jnp.concatenate([keys, keys], 0), jnp.concatenate([high, low], 0)
            )


def marks_of(refs, width):
    first = [ref[pl.ds(width + 1, 1), :] for ref in refs]
    last = [ref[pl.ds(width + 2, 1), :] for ref in refs]
    return first, last


def total_kernel(width, pairs, with_marks, count, *refs):
    marked, slots, out = refs[:count], refs[-1 - count : -1], refs[-1]
    last = marks_of(marked, width)[1]
    newest = functools.reduce(jnp.maximum, last)
    out[...] = total([slot[...] * (one == newest).astype(jnp.float32) for slot, one in zip(slots, last)])
    if with_marks:
        for pair in range(pairs):
            out[pl.ds(pair * (width + EXTRA) + width + 1, 2), :] = jnp.concatenate([newest, newest], 0)


def prefix_kernel(width, count, steps, me_ref, *refs):
    outs, refs = refs[-count:], refs[:-count]
    marked, marked_carries = refs[:count], refs[count : count + steps]
    slots, carries = refs[-count - steps : len(refs) - steps], refs[len(refs) - steps :]
    first, last = marks_of(marked, width)
    oldest = functools.reduce(jnp.minimum, first)
    carry_last = marks_of(marked_carries, width)[1]
    carry = total([one[...] * (mark == oldest).astype(jnp.float32) for one, mark in zip(carries, carry_last)])
    me = me_ref[0]
    for target, out in enumerate(outs):
        terms = [carry * (first[target] == oldest).astype(jnp.float32)]
        for source in range(count):
            if source != target:
                before = jnp.where((me ^ source) < (me ^ target), 1.0, 0.0)
                terms.append(slots[source][...] * ((last[source] == first[target]).astype(jnp.float32) * before))
        out[...] = total(terms)


def solve_kernel(width, pairs, count, me_ref, ridge_ref, ids_ref, q_ref, k_ref, v_ref, *refs):
    slots, (x_ref, near_ref) = refs[:count], refs[count:]
    upper, diagonal = triangle(width)
    ids = ids_ref[...].astype(jnp.float32)
    column = down(ids)
    rows = ids.shape[1]
    carried = jnp.broadcast_to((column == jnp.min(ids, 1, keepdims=True)).astype(jnp.float32), (rows, width))
    row_at = lax.broadcasted_iota(jnp.int32, (rows, rows), 0)
    col_at = lax.broadcasted_iota(jnp.int32, (rows, rows), 1)
    within = jnp.where(row_at >= col_at, (column == ids).astype(jnp.float32), 0.0)

    def scores(vector, turned, mask):
        return split(dot(vector, turned) * mask)

    for slot, state in enumerate(slots):
        group = []
        for pair in range(pairs):
            top = pair * (width + EXTRA)
            packed = state[pl.ds(top, width), :]
            flipped = packed.T
            second = state[pl.ds(top + width, 1), :]
            grams = [
                jnp.where(upper, packed, flipped),
                jnp.where(diagonal, second, jnp.where(upper, flipped, packed)),
            ]
            for side in range(2):
                head = ((me_ref[0] ^ slot) * pairs + pair) * 2 + side
                lanes = pl.ds(pl.multiple_of(head * width, width), width)
                wide = q_ref[:, lanes].astype(jnp.float32)
                query = wide * row_scale(wide)
                keys = k_ref[:, lanes]
                turned = keys.astype(jnp.float32).T
                scale = lax.rsqrt(jnp.sum(turned * turned, 0, keepdims=True) + 1e-06)
                turned = turned.astype(jnp.bfloat16)
                high, low = split(grams[side])
                both = jnp.concatenate([high, turned], 1)
                group.append(
                    dict(
                        lanes=lanes,
                        both=jnp.concatenate([both, both], 0),
                        low=low,
                        turned=jnp.concatenate([turned, turned], 0),
                        keys=jnp.concatenate([keys, keys], 0),
                        once=within * scale,
                        twice=within * (scale * scale),
                        ridge=ridge_ref[head],
                        remain=query,
                        search=query,
                        square=jnp.sum(query * query, -1, keepdims=True),
                    )
                )
        for step in range(CG_ITERS):
            for h in group:
                high, low = split(h["search"])
                wide = dot(jnp.concatenate([high, low], 1), h["both"])
                h["state"] = wide[:, :width] + dot(high, h["low"])
                h["score"] = split(wide[:, width:] * h["twice"])
            for h in group:
                local = dot(jnp.concatenate(h["score"], 1), h["keys"])
                search = h["search"]
                applied = h["state"] * carried + local + h["ridge"] * search
                size = h["square"] / jnp.sum(search * applied, -1, keepdims=True)
                h["solved"] = size * search if step == 0 else h["solved"] + size * search
                if step < CG_ITERS - 1:
                    remain = h["remain"] - size * applied
                    square = jnp.sum(remain * remain, -1, keepdims=True)
                    h["search"] = remain + square / h["square"] * search
                    h["remain"], h["square"] = remain, square
        for h in group:
            high, low = split(h["solved"])
            h["score"] = split(dot(jnp.concatenate([high, low], 1), h["turned"]) * h["once"])
            x_ref[:, h["lanes"]] = h["solved"] * carried
        for h in group:
            values = v_ref[:, h["lanes"]]
            near_ref[:, h["lanes"]] = dot(jnp.concatenate(h["score"], 1), jnp.concatenate([values, values], 0))


def readout_kernel(width, heads, count, me_ref, x_ref, near_ref, *refs):
    slots, out = refs[:count], refs[count]
    for slot, state in enumerate(slots):
        for head in range(heads):
            lanes = pl.ds(pl.multiple_of(((me_ref[0] ^ slot) * heads + head) * width, width), width)
            high, low = split(x_ref[:, lanes])
            s_high, s_low = split(state[pl.ds(head * width, width), :])
            far = dot(jnp.concatenate([high, low], 1), jnp.concatenate([s_high, s_high], 0)) + dot(high, s_low)
            out[:, lanes] = near_ref[:, lanes] + far


VMEM = pl.BlockSpec(memory_space=pltpu.VMEM)
SMEM = pl.BlockSpec(memory_space=pltpu.SMEM)
ANY = pl.BlockSpec(memory_space=pl.ANY)
PARAMS = pltpu.CompilerParams(vmem_limit_bytes=40 * 1024 * 1024)


def call(kernel, name, flops, out_shape, in_specs, arguments, scratch=()):
    out_specs = [VMEM] * len(out_shape) if isinstance(out_shape, list) else VMEM
    return pl.pallas_call(
        kernel,
        out_shape=out_shape,
        in_specs=in_specs,
        out_specs=out_specs,
        scratch_shapes=scratch,
        compiler_params=PARAMS,
        cost_estimate=pl.CostEstimate(flops=flops, bytes_accessed=0, transcendentals=0),
        name=name,
    )(*arguments)


def on_device(queries, key_vectors, value_vectors, segment_ids, ridge_weight):
    row_count, columns = queries.shape
    head_count = ridge_weight.shape[0]
    width = columns // head_count
    outer, half, near = lax.axis_size("outer"), lax.axis_size("half"), lax.axis_size("near")
    blocks = outer * half
    heads = head_count // near
    pairs = heads // 2
    steps = min(-(-(row_count * near * blocks // DOC_SHARE - 1) // (row_count * near)), blocks - 1)
    me = lax.axis_index("near").astype(jnp.int32).reshape(1)
    ids = segment_ids.reshape(1, row_count)
    gram_shape = jax.ShapeDtypeStruct((pairs * (width + EXTRA), width), jnp.float32)
    cross_shape = jax.ShapeDtypeStruct((heads * width, width), jnp.float32)
    unit = 32 * head_count * width * width * row_count
    flat = jax.ShapeDtypeStruct((row_count, columns), jnp.float32)

    def exchange(slots):
        return [slots[0]] + [
            lax.ppermute(slots[j], "near", [(i, i ^ j) for i in range(near)]) for j in range(1, near)
        ]

    def onward(value):
        return [
            lax.ppermute(value, ("outer", "half"), [(i, i + step) for i in range(blocks - step)])
            for step in range(1, steps + 1)
        ]

    own_gram = call(
        functools.partial(own_gram_kernel, width, pairs),
        "own_gram",
        unit,
        [gram_shape] * near,
        [SMEM, VMEM, ANY],
        (me, ids, key_vectors),
        (pltpu.VMEM((near, row_count, heads * width), key_vectors.dtype), pltpu.SemaphoreType.DMA((near,))),
    )
    gram = exchange(own_gram)
    own_cross = call(
        functools.partial(own_cross_kernel, width, heads),
        "own_cross",
        unit,
        [cross_shape] * near,
        [SMEM, VMEM, VMEM, VMEM],
        (me, ids, key_vectors, value_vectors),
    )
    cross = exchange(own_cross)
    gram_carry = onward(
        call(functools.partial(total_kernel, width, pairs, True, near), "gram_total", unit // 4, gram_shape, [VMEM] * near, gram)
    )
    cross_carry = onward(
        call(
            functools.partial(total_kernel, width, pairs, False, near),
            "cross_total",
        unit // 4,
            cross_shape,
            [VMEM] * (2 * near),
            (*gram, *cross),
        )
    )
    gram_prefix = exchange(
        call(
            functools.partial(prefix_kernel, width, near, steps),
            "gram_prefix",
        unit // 4,
            [gram_shape] * near,
            [SMEM] + [VMEM] * (near + steps),
            (me, *gram, *gram_carry),
        )
    )
    cross_prefix = exchange(
        call(
            functools.partial(prefix_kernel, width, near, steps),
            "cross_prefix",
        unit // 4,
            [cross_shape] * near,
            [SMEM] + [VMEM] * (2 * (near + steps)),
            (me, *gram, *gram_carry, *cross, *cross_carry),
        )
    )
    solved, local = call(
        functools.partial(solve_kernel, width, pairs, near),
        "solve",
        8 * unit,
        [flat, flat],
        [SMEM, SMEM, VMEM, VMEM, VMEM, VMEM] + [VMEM] * near,
        (me, ridge_weight, ids, queries, key_vectors, value_vectors, *gram_prefix),
    )
    return call(
        functools.partial(readout_kernel, width, heads, near),
        "readout",
        2 * unit,
        flat,
        [SMEM, VMEM, VMEM] + [VMEM] * near,
        (me, solved, local, *cross_prefix),
    )


def solution(mesh):
    outer, inner = mesh.shape["outer"], mesh.shape["inner"]
    near = inner // 2
    finer = Mesh(mesh.devices.reshape(outer, 2, near), ("outer", "half", "near"))
    tokens = P(("outer", "half", "near"))
    return jax.shard_map(
        on_device, mesh=finer, in_specs=(tokens, tokens, tokens, tokens, P()), out_specs=tokens, check_vma=False
    )
```

```python
import functools

import jax
import jax.numpy as jnp
from jax import lax
from jax.experimental import pallas as pl
from jax.experimental.pallas import tpu as pltpu
from jax.sharding import Mesh
from jax.sharding import PartitionSpec as P

CG_ITERS = 3
DOC_SHARE = 4
EXTRA = 8


def split(x):
    high = x.astype(jnp.bfloat16)
    low = (x - high.astype(jnp.float32)).astype(jnp.bfloat16)
    return high, low


def dot(a, b):
    return lax.dot_general(a, b, (((1,), (0,)), ((), ())), preferred_element_type=jnp.float32)


def dot_rows(a, b):
    return lax.dot_general(a, b, (((0,), (0,)), ((), ())), preferred_element_type=jnp.float32)


def total(terms):
    return functools.reduce(lambda a, b: a + b, terms)


def triangle(width):
    row = lax.broadcasted_iota(jnp.int32, (width, width), 0)
    col = lax.broadcasted_iota(jnp.int32, (width, width), 1)
    return row <= col, row == col


def down(ids):
    count = ids.shape[1]
    return jnp.broadcast_to(ids, (count, count)).T[:, :1]


def last_weight(ids_ref, width):
    ids = ids_ref[...].astype(jnp.float32)
    newest = jnp.max(ids, 1, keepdims=True)
    weight = (down(ids) == newest).astype(jnp.float32)
    return ids, newest, jnp.broadcast_to(weight, (ids.shape[1], width))


def row_scale(wide):
    return lax.rsqrt(jnp.sum(wide * wide, -1, keepdims=True) + 1e-06)


def own_kernel(base, width, pairs, count, me_ref, ids_ref, k_ref, v_ref, *refs):
    outs = refs[-count:]
    upper, diagonal = triangle(width)
    ids, newest, weight = last_weight(ids_ref, width)
    oldest = jnp.min(ids, 1, keepdims=True)
    marks = [jnp.broadcast_to(one + 1.0, (1, width)) for one in (oldest, newest)]
    filler = jnp.zeros((EXTRA - 3, width), jnp.float32)
    for slot, out in enumerate(outs):
        for pair in range(pairs):
            top = pair * (3 * width + EXTRA)
            grams = []
            for side in range(2):
                head = base + ((me_ref[0] ^ slot) * pairs + pair) * 2 + side
                lanes = pl.ds(pl.multiple_of(head * width, width), width)
                keys = k_ref[:, lanes]
                wide = keys.astype(jnp.float32)
                scale = row_scale(wide)
                light = weight * scale
                k_high, k_low = split(light * scale * wide)
                v_high, v_low = split(light * v_ref[:, lanes].astype(jnp.float32))
                right = jnp.concatenate(
                    [jnp.concatenate([k_high, v_high], 1), jnp.concatenate([k_low, v_low], 1)], 0
                )
                both = dot_rows(jnp.concatenate([keys, keys], 0), right)
                grams.append(both[:, :width])
                out[pl.ds(top + (1 + side) * width + EXTRA, width), :] = both[:, width:]
            out[pl.ds(top, width), :] = jnp.where(upper, grams[0], grams[1])
            second = jnp.sum(jnp.where(diagonal, grams[1], 0.0), 0, keepdims=True)
            out[pl.ds(top + width, EXTRA), :] = jnp.concatenate([second, *marks, filler], 0)


def marks_of(refs, width):
    first = [ref[pl.ds(width + 1, 1), :] for ref in refs]
    last = [ref[pl.ds(width + 2, 1), :] for ref in refs]
    return first, last


def total_kernel(width, pairs, count, *refs):
    slots, out = refs[:count], refs[-1]
    last = marks_of(slots, width)[1]
    newest = functools.reduce(jnp.maximum, last)
    out[...] = total([slot[...] * (one == newest).astype(jnp.float32) for slot, one in zip(slots, last)])
    for pair in range(pairs):
        out[pl.ds(pair * (3 * width + EXTRA) + width + 1, 2), :] = jnp.concatenate([newest, newest], 0)


def prefix_kernel(width, count, me_ref, *refs):
    slots, carries, outs = refs[:count], refs[count:-count], refs[-count:]
    first, last = marks_of(slots, width)
    oldest = functools.reduce(jnp.minimum, first)
    carry_last = marks_of(carries, width)[1]
    carry = total([one[...] * (mark == oldest).astype(jnp.float32) for one, mark in zip(carries, carry_last)])
    me = me_ref[0]
    for target, out in enumerate(outs):
        terms = [carry * (first[target] == oldest).astype(jnp.float32)]
        for source in range(count):
            if source != target:
                before = jnp.where((me ^ source) < (me ^ target), 1.0, 0.0)
                terms.append(slots[source][...] * ((last[source] == first[target]).astype(jnp.float32) * before))
        out[...] = total(terms)


def solve_kernel(base, width, pairs, count, me_ref, ridge_ref, ids_ref, q_ref, k_ref, v_ref, *refs):
    slots, out = refs[:count], refs[-1]
    upper, diagonal = triangle(width)
    ids = ids_ref[...].astype(jnp.float32)
    column = down(ids)
    rows = ids.shape[1]
    carried = jnp.broadcast_to((column == jnp.min(ids, 1, keepdims=True)).astype(jnp.float32), (rows, width))
    row_at = lax.broadcasted_iota(jnp.int32, (rows, rows), 0)
    col_at = lax.broadcasted_iota(jnp.int32, (rows, rows), 1)
    within = jnp.where(row_at >= col_at, (column == ids).astype(jnp.float32), 0.0)

    group = []
    for slot, state in enumerate(slots):
        for pair in range(pairs):
            top = pair * (3 * width + EXTRA)
            packed = state[pl.ds(top, width), :]
            flipped = packed.T
            second = state[pl.ds(top + width, 1), :]
            grams = [
                jnp.where(upper, packed, flipped),
                jnp.where(diagonal, second, jnp.where(upper, flipped, packed)),
            ]
            for side in range(2):
                local = ((me_ref[0] ^ slot) * pairs + pair) * 2 + side
                head = base + local
                lanes = pl.ds(pl.multiple_of(head * width, width), width)
                wide = q_ref[:, lanes].astype(jnp.float32)
                query = wide * row_scale(wide)
                keys = k_ref[:, lanes]
                turned = keys.astype(jnp.float32).T
                scale = lax.rsqrt(jnp.sum(turned * turned, 0, keepdims=True) + 1e-06)
                turned = turned.astype(jnp.bfloat16)
                high, low = split(grams[side])
                both = jnp.concatenate([high, turned], 1)
                group.append(
                    dict(
                        lanes=lanes,
                        place=pl.ds(pl.multiple_of(local * width, width), width),
                        cross=state.at[pl.ds(top + EXTRA + (1 + side) * width, width)],
                        both=jnp.concatenate([both, both], 0),
                        low=low,
                        turned=turned,
                        keys=jnp.concatenate([keys, keys], 0),
                        once=within * scale,
                        twice=within * (scale * scale),
                        ridge=ridge_ref[head],
                        remain=query,
                        search=query,
                        square=jnp.sum(query * query, -1, keepdims=True),
                    )
                )
    for step in range(CG_ITERS):
        for h in group:
            high, low = split(h["search"])
            wide = dot(jnp.concatenate([high, low], 1), h["both"])
            h["state"] = wide[:, :width] + dot(high, h["low"])
            h["score"] = split(wide[:, width:] * h["twice"])
        for h in group:
            local = dot(jnp.concatenate(h["score"], 1), h["keys"])
            search = h["search"]
            applied = h["state"] * carried + local + h["ridge"] * search
            size = h["square"] / jnp.sum(search * applied, -1, keepdims=True)
            h["solved"] = size * search if step == 0 else h["solved"] + size * search
            if step < CG_ITERS - 1:
                remain = h["remain"] - size * applied
                square = jnp.sum(remain * remain, -1, keepdims=True)
                h["search"] = remain + square / h["square"] * search
                h["remain"], h["square"] = remain, square
    for h in group:
        high, low = split(h["solved"])
        c_high, c_low = split(h["cross"][...])
        both = jnp.concatenate([c_high, h["turned"]], 1)
        wide = dot(jnp.concatenate([high, low], 1), jnp.concatenate([both, both], 0))
        h["state"] = wide[:, :width] + dot(high, c_low)
        h["score"] = split(wide[:, width:] * h["once"])
    for h in group:
        values = v_ref[:, h["lanes"]]
        local = dot(jnp.concatenate(h["score"], 1), jnp.concatenate([values, values], 0))
        out[:, h["place"]] = h["state"] * carried + local


VMEM = pl.BlockSpec(memory_space=pltpu.VMEM)
SMEM = pl.BlockSpec(memory_space=pltpu.SMEM)
ANY = pl.BlockSpec(memory_space=pl.ANY)
PARAMS = pltpu.CompilerParams(vmem_limit_bytes=40 * 1024 * 1024)


def call(kernel, name, flops, out_shape, in_specs, arguments, **more):
    out_specs = [VMEM] * len(out_shape) if isinstance(out_shape, list) else VMEM
    return pl.pallas_call(
        kernel,
        out_shape=out_shape,
        in_specs=in_specs,
        compiler_params=PARAMS,
        cost_estimate=pl.CostEstimate(flops=flops, bytes_accessed=0, transcendentals=0),
        name=name,
        **{"out_specs": out_specs, **more},
    )(*arguments)


def on_device(queries, key_vectors, value_vectors, segment_ids, ridge_weight, *, pieces):
    row_count, columns = queries.shape
    head_count = ridge_weight.shape[0]
    width = columns // head_count
    outer, half, near = lax.axis_size("outer"), lax.axis_size("half"), lax.axis_size("near")
    blocks = outer * half
    pairs = head_count // (2 * near * pieces)
    steps = min(-(-(row_count * near * blocks // DOC_SHARE - 1) // (row_count * near)), blocks - 1)
    me = lax.axis_index("near").astype(jnp.int32).reshape(1)
    ids = segment_ids.reshape(1, row_count)
    shape = jax.ShapeDtypeStruct((pairs * (3 * width + EXTRA), width), jnp.float32)
    unit = 32 * pairs * 2 * near * width * width * row_count

    def exchange(slots):
        return [slots[0]] + [
            lax.ppermute(slots[j], "near", [(i, i ^ j) for i in range(near)]) for j in range(1, near)
        ]

    def onward(value):
        return [
            lax.ppermute(value, ("outer", "half"), [(i, i + step) for i in range(blocks - step)])
            for step in range(1, steps + 1)
        ]

    states = []
    for piece in range(pieces):
        own = call(
            functools.partial(own_kernel, piece * pairs * near * 2, width, pairs, near),
            "own_sums",
            unit,
            [shape] * near,
            [SMEM, VMEM, VMEM, VMEM],
            (me, ids, key_vectors, value_vectors),
        )
        slots = exchange(own)
        block_total = call(
            functools.partial(total_kernel, width, pairs, near), "block_total", unit // 4, shape, [VMEM] * near, slots
        )
        prefix = call(
            functools.partial(prefix_kernel, width, near),
            "prefixes",
            unit // 4,
            [shape] * near,
            [SMEM] + [VMEM] * (near + steps),
            (me, *slots, *onward(block_total)),
        )
        states.append(exchange(prefix))
    out = None
    for piece, state in enumerate(states):
        base = piece * pairs * near * 2
        span = pairs * near * 2 * width
        arguments = [me, ridge_weight, ids, queries, key_vectors, value_vectors, *state]
        in_specs = [SMEM, SMEM, VMEM, VMEM, VMEM, VMEM] + [VMEM] * near
        aliases = {}
        if out is not None:
            aliases = {len(arguments): 0}
            arguments.append(out)
            in_specs.append(ANY)
        out = call(
            functools.partial(solve_kernel, base, width, pairs, near),
            "solve",
            8 * unit,
            jax.ShapeDtypeStruct((row_count, columns), jnp.float32),
            in_specs,
            arguments,
            grid=(1,),
            out_specs=pl.BlockSpec((row_count, span), functools.partial(lambda p, i: (0, p), piece)),
            input_output_aliases=aliases,
        )
    return out


def solution(mesh):
    outer, inner = mesh.shape["outer"], mesh.shape["inner"]
    near = inner // 2
    finer = Mesh(mesh.devices.reshape(outer, 2, near), ("outer", "half", "near"))
    tokens = P(("outer", "half", "near"))

    def run(*arguments):
        pieces = max(1, min(2, arguments[-1].shape[0] // (2 * near)))
        return jax.shard_map(
            functools.partial(on_device, pieces=pieces),
            mesh=finer,
            in_specs=(tokens, tokens, tokens, tokens, P()),
            out_specs=tokens,
            check_vma=False,
        )(*arguments)

    return run
```

```python
import functools

import jax
import jax.numpy as jnp
from jax import lax
from jax.experimental import pallas as pl
from jax.experimental.pallas import tpu as pltpu
from jax.sharding import Mesh
from jax.sharding import PartitionSpec as P

CG_ITERS = 3
DOC_SHARE = 4
EXTRA = 8


def split(x):
    high = x.astype(jnp.bfloat16)
    low = (x - high.astype(jnp.float32)).astype(jnp.bfloat16)
    return high, low


def dot(a, b):
    return lax.dot_general(a, b, (((1,), (0,)), ((), ())), preferred_element_type=jnp.float32)


def dot_rows(a, b):
    return lax.dot_general(a, b, (((0,), (0,)), ((), ())), preferred_element_type=jnp.float32)


def total(terms):
    return functools.reduce(lambda a, b: a + b, terms)


def triangle(width):
    row = lax.broadcasted_iota(jnp.int32, (width, width), 0)
    col = lax.broadcasted_iota(jnp.int32, (width, width), 1)
    return row <= col, row == col


def down(ids):
    count = ids.shape[1]
    return jnp.broadcast_to(ids, (count, count)).T[:, :1]


def row_scale(wide):
    return lax.rsqrt(jnp.sum(wide * wide, -1, keepdims=True) + 1e-06)


def own_kernel(base, width, pairs, count, me_ref, ids_ref, k_ref, v_ref, *refs):
    outs, scratch = refs[:count], refs[count:]
    span = pairs * 2 * width
    spans = [pl.ds(pl.multiple_of(base * width + (me_ref[0] ^ slot) * span, span), span) for slot in range(count)]
    copies = []
    if scratch:
        ids_to, k_to, v_to, sems = scratch
        moves = [(ids_ref, ids_to)]
        for slot in range(count):
            moves += [(k_ref.at[:, spans[slot]], k_to.at[slot]), (v_ref.at[:, spans[slot]], v_to.at[slot])]
        copies = [pltpu.make_async_copy(*move, sems.at[number]) for number, move in enumerate(moves)]
        for copy in copies:
            copy.start()
        ids_ref, k_parts, v_parts = ids_to, [k_to.at[slot] for slot in range(count)], [v_to.at[slot] for slot in range(count)]
    else:
        k_parts, v_parts = ([ref.at[:, one] for one in spans] for ref in (k_ref, v_ref))
    upper, diagonal = triangle(width)
    for copy in copies[:1]:
        copy.wait()
    ids = ids_ref[...].astype(jnp.float32)
    oldest, newest = jnp.min(ids, 1, keepdims=True), jnp.max(ids, 1, keepdims=True)
    weight = jnp.broadcast_to((down(ids) == newest).astype(jnp.float32), (ids.shape[1], width))
    marks = [jnp.broadcast_to(one + 1.0, (1, width)) for one in (oldest, newest)]
    filler = jnp.zeros((EXTRA - 3, width), jnp.float32)
    for slot, out in enumerate(outs):
        for copy in copies[1 + 2 * slot : 3 + 2 * slot]:
            copy.wait()
        for pair in range(pairs):
            top = pair * (3 * width + EXTRA)
            grams = []
            for side in range(2):
                lanes = pl.ds((pair * 2 + side) * width, width)
                keys = k_parts[slot][:, lanes]
                wide = keys.astype(jnp.float32)
                scale = row_scale(wide)
                light = weight * scale
                k_high, k_low = split(light * scale * wide)
                v_high, v_low = split(light * v_parts[slot][:, lanes].astype(jnp.float32))
                right = jnp.concatenate(
                    [jnp.concatenate([k_high, v_high], 1), jnp.concatenate([k_low, v_low], 1)], 0
                )
                both = dot_rows(jnp.concatenate([keys, keys], 0), right)
                grams.append(both[:, :width])
                out[pl.ds(top + (1 + side) * width + EXTRA, width), :] = both[:, width:]
            out[pl.ds(top, width), :] = jnp.where(upper, grams[0], grams[1])
            second = jnp.sum(jnp.where(diagonal, grams[1], 0.0), 0, keepdims=True)
            out[pl.ds(top + width, EXTRA), :] = jnp.concatenate([second, *marks, filler], 0)


def marks_of(refs, width):
    first = [ref[pl.ds(width + 1, 1), :] for ref in refs]
    last = [ref[pl.ds(width + 2, 1), :] for ref in refs]
    return first, last


def total_kernel(width, pairs, count, *refs):
    slots, out = refs[:count], refs[-1]
    last = marks_of(slots, width)[1]
    newest = functools.reduce(jnp.maximum, last)
    out[...] = total([slot[...] * (one == newest).astype(jnp.float32) for slot, one in zip(slots, last)])
    for pair in range(pairs):
        out[pl.ds(pair * (3 * width + EXTRA) + width + 1, 2), :] = jnp.concatenate([newest, newest], 0)


def prefix_kernel(width, count, me_ref, *refs):
    slots, carries, outs = refs[:count], refs[count:-count], refs[-count:]
    first, last = marks_of(slots, width)
    oldest = functools.reduce(jnp.minimum, first)
    carry_last = marks_of(carries, width)[1]
    carry = total([one[...] * (mark == oldest).astype(jnp.float32) for one, mark in zip(carries, carry_last)])
    me = me_ref[0]
    for target, out in enumerate(outs):
        terms = [carry * (first[target] == oldest).astype(jnp.float32)]
        for source in range(count):
            if source != target:
                before = jnp.where((me ^ source) < (me ^ target), 1.0, 0.0)
                terms.append(slots[source][...] * ((last[source] == first[target]).astype(jnp.float32) * before))
        out[...] = total(terms)


def solve_kernel(places, width, pairs, me_ref, ridge_ref, ids_ref, q_ref, k_ref, v_ref, *refs):
    slots, (out_hbm, out, sems) = refs[: len(places)], refs[-3:]
    upper, diagonal = triangle(width)
    ids = ids_ref[...].astype(jnp.float32)
    column = down(ids)
    rows = ids.shape[1]
    carried = jnp.broadcast_to((column == jnp.min(ids, 1, keepdims=True)).astype(jnp.float32), (rows, width))
    row_at = lax.broadcasted_iota(jnp.int32, (rows, rows), 0)
    col_at = lax.broadcasted_iota(jnp.int32, (rows, rows), 1)
    within = jnp.where(row_at >= col_at, (column == ids).astype(jnp.float32), 0.0)

    group = []
    for (base, slot), state in zip(places, slots):
        for pair in range(pairs):
            top = pair * (3 * width + EXTRA)
            packed = state[pl.ds(top, width), :]
            flipped = packed.T
            second = state[pl.ds(top + width, 1), :]
            grams = [
                jnp.where(upper, packed, flipped),
                jnp.where(diagonal, second, jnp.where(upper, flipped, packed)),
            ]
            for side in range(2):
                head = base + ((me_ref[0] ^ slot) * pairs + pair) * 2 + side
                lanes = pl.ds(pl.multiple_of(head * width, width), width)
                wide = q_ref[:, lanes].astype(jnp.float32)
                query = wide * row_scale(wide)
                keys = k_ref[:, lanes]
                turned = keys.astype(jnp.float32).T
                scale = lax.rsqrt(jnp.sum(turned * turned, 0, keepdims=True) + 1e-06)
                turned = turned.astype(jnp.bfloat16)
                high, low = split(grams[side])
                both = jnp.concatenate([high, turned], 1)
                group.append(
                    dict(
                        lanes=lanes,
                        cross=state.at[pl.ds(top + EXTRA + (1 + side) * width, width)],
                        both=jnp.concatenate([both, both], 0),
                        low=low,
                        turned=turned,
                        keys=jnp.concatenate([keys, keys], 0),
                        once=within * scale,
                        twice=within * (scale * scale),
                        ridge=ridge_ref[head],
                        remain=query,
                        search=query,
                        square=jnp.sum(query * query, -1, keepdims=True),
                    )
                )
    for step in range(CG_ITERS):
        for h in group:
            high, low = split(h["search"])
            wide = dot(jnp.concatenate([high, low], 1), h["both"])
            h["state"] = wide[:, :width] + dot(high, h["low"])
            h["score"] = split(wide[:, width:] * h["twice"])
        for h in group:
            local = dot(jnp.concatenate(h["score"], 1), h["keys"])
            search = h["search"]
            applied = h["state"] * carried + local + h["ridge"] * search
            size = h["square"] / jnp.sum(search * applied, -1, keepdims=True)
            h["solved"] = size * search if step == 0 else h["solved"] + size * search
            if step < CG_ITERS - 1:
                remain = h["remain"] - size * applied
                square = jnp.sum(remain * remain, -1, keepdims=True)
                h["search"] = remain + square / h["square"] * search
                h["remain"], h["square"] = remain, square
    for h in group:
        high, low = split(h["solved"])
        c_high, c_low = split(h["cross"][...])
        both = jnp.concatenate([c_high, h["turned"]], 1)
        wide = dot(jnp.concatenate([high, low], 1), jnp.concatenate([both, both], 0))
        h["state"] = wide[:, :width] + dot(high, c_low)
        h["score"] = split(wide[:, width:] * h["once"])
    copies = []
    for number, h in enumerate(group):
        values = v_ref[:, h["lanes"]]
        local = dot(jnp.concatenate(h["score"], 1), jnp.concatenate([values, values], 0))
        out[number] = h["state"] * carried + local
        copies.append(pltpu.make_async_copy(out.at[number], out_hbm.at[:, h["lanes"]], sems.at[number]))
        copies[-1].start()
    for copy in copies:
        copy.wait()


VMEM = pl.BlockSpec(memory_space=pltpu.VMEM)
SMEM = pl.BlockSpec(memory_space=pltpu.SMEM)
HBM = pl.BlockSpec(memory_space=pltpu.HBM)
PARAMS = pltpu.CompilerParams(vmem_limit_bytes=40 * 1024 * 1024)


def call(kernel, name, flops, out_shape, in_specs, arguments, **more):
    out_specs = [VMEM] * len(out_shape) if isinstance(out_shape, list) else VMEM
    return pl.pallas_call(
        kernel,
        out_shape=out_shape,
        in_specs=in_specs,
        compiler_params=PARAMS,
        cost_estimate=pl.CostEstimate(flops=flops, bytes_accessed=0, transcendentals=0),
        name=name,
        **{"out_specs": out_specs, **more},
    )(*arguments)


def on_device(queries, key_vectors, value_vectors, segment_ids, ridge_weight, *, pieces):
    row_count, columns = queries.shape
    head_count = ridge_weight.shape[0]
    width = columns // head_count
    outer, half, near = lax.axis_size("outer"), lax.axis_size("half"), lax.axis_size("near")
    blocks = outer * half
    pairs = head_count // (2 * near * pieces)
    steps = min(-(-(row_count * near * blocks // DOC_SHARE - 1) // (row_count * near)), blocks - 1)
    me = lax.axis_index("near").astype(jnp.int32).reshape(1)
    ids = segment_ids.reshape(1, row_count)
    shape = jax.ShapeDtypeStruct((pairs * (3 * width + EXTRA), width), jnp.float32)
    unit = 32 * pairs * 2 * near * width * width * row_count

    def exchange(slots):
        return [slots[0]] + [
            lax.ppermute(slots[j], "near", [(i, i ^ j) for i in range(near)]) for j in range(1, near)
        ]

    def onward(value):
        return [
            lax.ppermute(value, ("outer", "half"), [(i, (i + step) % blocks) for i in range(blocks)])
            for step in range(1, steps + 1)
        ]

    states = []
    tokens = (ids, key_vectors, value_vectors)
    part = (near, row_count, 2 * pairs * width)
    for piece in range(pieces):
        first = piece == 0
        scratch = [
            pltpu.VMEM(ids.shape, ids.dtype),
            pltpu.VMEM(part, key_vectors.dtype),
            pltpu.VMEM(part, value_vectors.dtype),
            pltpu.SemaphoreType.DMA((2 * near + 1,)),
        ]
        own = call(
            functools.partial(own_kernel, piece * pairs * near * 2, width, pairs, near),
            "own_sums",
            unit,
            [shape] * near,
            [SMEM] + [HBM if first else VMEM] * 3,
            (me, *[pltpu.with_memory_space_constraint(one, pltpu.HBM) if first else one for one in tokens]),
            scratch_shapes=scratch if first else [],
        )
        slots = exchange(own)
        block_total = call(
            functools.partial(total_kernel, width, pairs, near), "block_total", unit // 4, shape, [VMEM] * near, slots
        )
        prefix = call(
            functools.partial(prefix_kernel, width, near),
            "prefixes",
            unit // 4,
            [shape] * near,
            [SMEM] + [VMEM] * (near + steps),
            (me, *slots, *onward(block_total)),
        )
        states.append(exchange(prefix))
    out = None
    for piece, state in enumerate(states):
        places = [(piece * pairs * near * 2, slot) for slot in range(near)]
        arguments = [me, ridge_weight, ids, queries, key_vectors, value_vectors, *state]
        in_specs = [SMEM, SMEM, VMEM, VMEM, VMEM, VMEM] + [VMEM] * near
        aliases = {}
        if out is not None:
            aliases = {len(arguments): 0}
            arguments.append(out)
            in_specs.append(HBM)
        count = 2 * pairs * near
        out = call(
            functools.partial(solve_kernel, places, width, pairs),
            "solve",
            8 * unit,
            jax.ShapeDtypeStruct((row_count, columns), jnp.float32),
            in_specs,
            arguments,
            out_specs=HBM,
            scratch_shapes=[pltpu.VMEM((count, row_count, width), jnp.float32), pltpu.SemaphoreType.DMA((count,))],
            input_output_aliases=aliases,
        )
    return out


def solution(mesh):
    outer, inner = mesh.shape["outer"], mesh.shape["inner"]
    near = inner // 2
    finer = Mesh(mesh.devices.reshape(outer, 2, near), ("outer", "half", "near"))
    tokens = P(("outer", "half", "near"))

    def run(*arguments):
        pieces = max(1, min(2, arguments[-1].shape[0] // (2 * near)))
        return jax.shard_map(
            functools.partial(on_device, pieces=pieces),
            mesh=finer,
            in_specs=(tokens, tokens, tokens, tokens, P()),
            out_specs=tokens,
            check_vma=False,
        )(*arguments)

    return run
```

```python
import functools

import jax
import jax.numpy as jnp
from jax import lax
from jax.experimental import pallas as pl
from jax.experimental.pallas import tpu as pltpu
from jax.sharding import Mesh
from jax.sharding import PartitionSpec as P

CG_ITERS = 3
DOC_SHARE = 4


def split(x):
    high = x.astype(jnp.bfloat16)
    low = (x - high.astype(jnp.float32)).astype(jnp.bfloat16)
    return high, low


def dot(a, b):
    return lax.dot_general(a, b, (((1,), (0,)), ((), ())), preferred_element_type=jnp.float32)


def dot_rows(a, b):
    return lax.dot_general(a, b, (((0,), (0,)), ((), ())), preferred_element_type=jnp.float32)


def total(terms):
    return functools.reduce(lambda a, b: a + b, terms)


def triangle(width):
    row = lax.broadcasted_iota(jnp.int32, (width, width), 0)
    col = lax.broadcasted_iota(jnp.int32, (width, width), 1)
    return row <= col, row == col


def down(ids):
    count = ids.shape[1]
    return jnp.broadcast_to(ids, (count, count)).T[:, :1]


def row_scale(wide):
    return lax.rsqrt(jnp.sum(wide * wide, -1, keepdims=True) + 1e-06)


def extra_of(packs):
    return -(-(packs + 2) // 8) * 8


def last_of(ids_ref, width):
    ids = ids_ref[...].astype(jnp.float32)
    oldest, newest = jnp.min(ids, 1, keepdims=True), jnp.max(ids, 1, keepdims=True)
    weight = jnp.broadcast_to((down(ids) == newest).astype(jnp.float32), (ids.shape[1], width))
    return oldest, newest, weight


def own_first_kernel(width, packs, early, count, ids_hbm, k_hbm, v_hbm, *refs):
    outs, (ids_ref, k_ref, v_ref, sems) = refs[:count], refs[count:]
    span = 2 * packs * width
    moves = [(ids_hbm, ids_ref)]
    for slot in range(count):
        start = pl.multiple_of((lax.axis_index("near") ^ slot) * span, span)
        moves.append((k_hbm.at[:, pl.ds(start, span)], k_ref.at[slot]))
        if early:
            moves.append((v_hbm.at[:, pl.ds(start, early * width)], v_ref.at[slot]))
    copies = [pltpu.make_async_copy(*move, sems.at[number]) for number, move in enumerate(moves)]
    for copy in copies:
        copy.start()
    upper, diagonal = triangle(width)
    for copy in copies:
        copy.wait()
    oldest, newest, weight = last_of(ids_ref, width)
    marks = [jnp.broadcast_to(one + 1.0, (1, width)) for one in (oldest, newest)]
    extra = extra_of(packs)
    filler = jnp.zeros((extra - packs - 2, width), jnp.float32)
    for slot, out in enumerate(outs):
        grams = []
        for head in range(2 * packs):
            lanes = pl.ds(head * width, width)
            keys = k_ref[slot, :, lanes]
            wide = keys.astype(jnp.float32)
            scale = row_scale(wide)
            light = weight * scale
            high, low = split(light * scale * wide)
            if head < early:
                v_high, v_low = split(light * v_ref[slot, :, lanes].astype(jnp.float32))
                high, low = jnp.concatenate([high, v_high], 1), jnp.concatenate([low, v_low], 1)
            both = dot_rows(jnp.concatenate([keys, keys], 0), jnp.concatenate([high, low], 0))
            grams.append(both[:, :width])
            if head < early:
                out[pl.ds((packs + head) * width + extra, width), :] = both[:, width:]
        seconds = []
        for pack in range(packs):
            one, two = grams[2 * pack : 2 * pack + 2]
            out[pl.ds(pack * width, width), :] = jnp.where(upper, one, two)
            seconds.append(jnp.sum(jnp.where(diagonal, two, 0.0), 0, keepdims=True))
        out[pl.ds(packs * width, extra), :] = jnp.concatenate([*seconds, *marks, filler], 0)


def own_rest_kernel(width, heads, early, ids_ref, k_ref, v_ref, *outs):
    weight = last_of(ids_ref, width)[2]
    for slot, out in enumerate(outs):
        for head in range(early, heads):
            at = (lax.axis_index("near") ^ slot) * heads + head
            lanes = pl.ds(pl.multiple_of(at * width, width), width)
            keys = k_ref[:, lanes]
            scale = row_scale(keys.astype(jnp.float32))
            high, low = split(weight * scale * v_ref[:, lanes].astype(jnp.float32))
            out[pl.ds((head - early) * width, width), :] = dot_rows(
                jnp.concatenate([keys, keys], 0), jnp.concatenate([high, low], 0)
            )


def marks_of(refs, at):
    return [ref[pl.ds(at, 1), :] for ref in refs], [ref[pl.ds(at + 1, 1), :] for ref in refs]


def flag(condition):
    return condition.astype(jnp.float32)


def total_kernel(at, count, *refs):
    marked, slots, out = refs[:count], refs[-1 - count : -1], refs[-1]
    last = marks_of(marked, at)[1]
    newest = functools.reduce(jnp.maximum, last)
    out[...] = total([slot[...] * flag(one == newest) for slot, one in zip(slots, last)])
    if len(refs) == count + 1:
        out[pl.ds(at, 2), :] = jnp.concatenate([newest, newest], 0)


def prefix_kernel(at, count, steps, *refs):
    outs, refs = refs[-count:], refs[:-count]
    marked, marked_carries = refs[:count], refs[count : count + steps]
    slots, carries = refs[-count - steps : -steps], refs[-steps:]
    first, last = marks_of(marked, at)
    oldest = functools.reduce(jnp.minimum, first)
    ends = marks_of(marked_carries, at)[1]
    carry = total([one[...] * flag(mark == oldest) for one, mark in zip(carries, ends)])
    me = lax.axis_index("near")
    for target, out in enumerate(outs):
        terms = [carry * flag(first[target] == oldest)]
        for source in range(count):
            if source != target:
                before = jnp.where((me ^ source) < (me ^ target), 1.0, 0.0)
                terms.append(slots[source][...] * (flag(last[source] == first[target]) * before))
        out[...] = total(terms)


def far_part(pair, high, cross):
    c_high, c_low = split(cross)
    return dot(pair, jnp.concatenate([c_high, c_high], 0)) + dot(high, c_low)


def solve_kernel(width, packs, early, together, ridge_ref, ids_ref, q_ref, k_ref, v_ref, *refs):
    slots, (x_ref, near_ref, out_hbm, out, sems) = refs[:-5], refs[-5:]
    upper, diagonal = triangle(width)
    ids = ids_ref[...].astype(jnp.float32)
    column = down(ids)
    rows = ids.shape[1]
    carried = jnp.broadcast_to(flag(column == jnp.min(ids, 1, keepdims=True)), (rows, width))
    row_at = lax.broadcasted_iota(jnp.int32, (rows, rows), 0)
    col_at = lax.broadcasted_iota(jnp.int32, (rows, rows), 1)
    within = jnp.where(row_at >= col_at, flag(column == ids), 0.0)
    copies = []
    for start in range(0, len(slots), together):
        group = []
        for slot, pack in [(j, p) for j in range(start, min(start + together, len(slots))) for p in range(packs)]:
            state = slots[slot]
            packed = state[pl.ds(pack * width, width), :]
            flipped = packed.T
            second = state[pl.ds(packs * width + pack, 1), :]
            grams = [
                jnp.where(upper, packed, flipped),
                jnp.where(diagonal, second, jnp.where(upper, flipped, packed)),
            ]
            for side in range(2):
                head = ((lax.axis_index("near") ^ slot) * packs + pack) * 2 + side
                lanes = pl.ds(pl.multiple_of(head * width, width), width)
                wide = q_ref[:, lanes].astype(jnp.float32)
                query = wide * row_scale(wide)
                keys = k_ref[:, lanes]
                turned = keys.astype(jnp.float32).T
                scale = lax.rsqrt(jnp.sum(turned * turned, 0, keepdims=True) + 1e-06)
                turned = turned.astype(jnp.bfloat16)
                high, low = split(grams[side])
                both = jnp.concatenate([high, turned], 1)
                group.append(
                    dict(
                        lanes=lanes,
                        cross=state.at[pl.ds((packs + 2 * pack + side) * width + extra_of(packs), width)]
                        if 2 * pack + side < early
                        else None,
                        both=jnp.concatenate([both, both], 0),
                        low=low,
                        turned=jnp.concatenate([turned, turned], 0),
                        keys=jnp.concatenate([keys, keys], 0),
                        once=within * scale,
                        twice=within * (scale * scale),
                        ridge=ridge_ref[head],
                        remain=query,
                        search=query,
                        square=jnp.sum(query * query, -1, keepdims=True),
                    )
                )
        for step in range(CG_ITERS):
            for h in group:
                high, low = split(h["search"])
                wide = dot(jnp.concatenate([high, low], 1), h["both"])
                h["state"] = wide[:, :width] + dot(high, h["low"])
                h["score"] = split(wide[:, width:] * h["twice"])
            for h in group:
                local = dot(jnp.concatenate(h["score"], 1), h["keys"])
                search = h["search"]
                applied = h["state"] * carried + local + h["ridge"] * search
                size = h["square"] / jnp.sum(search * applied, -1, keepdims=True)
                h["solved"] = size * search if step == 0 else h["solved"] + size * search
                if step < CG_ITERS - 1:
                    remain = h["remain"] - size * applied
                    square = jnp.sum(remain * remain, -1, keepdims=True)
                    h["search"] = remain + square / h["square"] * search
                    h["remain"], h["square"] = remain, square
        for h in group:
            high, low = split(h["solved"])
            pair = jnp.concatenate([high, low], 1)
            h["score"] = split(dot(pair, h["turned"]) * h["once"])
            if h["cross"] is None:
                x_ref[:, h["lanes"]] = h["solved"] * carried
            else:
                h["far"] = far_part(pair, high, h["cross"][...]) * carried
        for h in group:
            values = v_ref[:, h["lanes"]]
            local = dot(jnp.concatenate(h["score"], 1), jnp.concatenate([values, values], 0))
            if h["cross"] is None:
                near_ref[:, h["lanes"]] = local
            else:
                at = len(copies)
                out[at] = local + h["far"]
                copies.append(pltpu.make_async_copy(out.at[at], out_hbm.at[:, h["lanes"]], sems.at[at]))
                copies[-1].start()
    for copy in copies:
        copy.wait()


def readout_kernel(width, heads, early, count, x_ref, near_ref, *refs):
    slots, (out_hbm, out, sems) = refs[:count], refs[-3:]
    copies = []
    for slot, state in enumerate(slots):
        for head in range(early, heads):
            at = (lax.axis_index("near") ^ slot) * heads + head
            lanes = pl.ds(pl.multiple_of(at * width, width), width)
            high, low = split(x_ref[:, lanes])
            far = far_part(jnp.concatenate([high, low], 1), high, state[pl.ds((head - early) * width, width), :])
            number = len(copies)
            out[number] = near_ref[:, lanes] + far
            copies.append(pltpu.make_async_copy(out.at[number], out_hbm.at[:, lanes], sems.at[number]))
            copies[-1].start()
    for copy in copies:
        copy.wait()


VMEM = pl.BlockSpec(memory_space=pltpu.VMEM)
SMEM = pl.BlockSpec(memory_space=pltpu.SMEM)
HBM = pl.BlockSpec(memory_space=pltpu.HBM)
PARAMS = pltpu.CompilerParams(vmem_limit_bytes=40 * 1024 * 1024)


def call(kernel, name, flops, out_shape, in_specs, arguments, **more):
    out_specs = [VMEM] * len(out_shape) if isinstance(out_shape, list) else VMEM
    return pl.pallas_call(
        kernel,
        out_shape=out_shape,
        in_specs=in_specs,
        compiler_params=PARAMS,
        cost_estimate=pl.CostEstimate(flops=flops, bytes_accessed=0, transcendentals=0),
        name=name,
        **{"out_specs": out_specs, **more},
    )(*arguments)


def on_device(queries, key_vectors, value_vectors, segment_ids, ridge_weight):
    row_count, columns = queries.shape
    head_count = ridge_weight.shape[0]
    width = columns // head_count
    outer, half, near = lax.axis_size("outer"), lax.axis_size("half"), lax.axis_size("near")
    blocks = outer * half
    heads = head_count // near
    packs = heads // 2
    early = heads // 4
    steps = min(-(-(row_count * near * blocks // DOC_SHARE - 1) // (row_count * near)), blocks - 1)
    ids = segment_ids.reshape(1, row_count)
    mark_at = packs * width + packs
    first_shape = jax.ShapeDtypeStruct(((packs + early) * width + extra_of(packs), width), jnp.float32)
    rest_shape = jax.ShapeDtypeStruct(((heads - early) * width, width), jnp.float32)
    flat = jax.ShapeDtypeStruct((row_count, columns), jnp.float32)
    unit = 16 * head_count * width * width * row_count

    def exchange(slots):
        return [slots[0]] + [
            lax.ppermute(slots[j], "near", [(i, i ^ j) for i in range(near)]) for j in range(1, near)
        ]

    def onward(value):
        return [
            lax.ppermute(value, ("outer", "half"), [(i, (i + step) % blocks) for i in range(blocks)])
            for step in range(1, steps + 1)
        ]

    own_first = call(
        functools.partial(own_first_kernel, width, packs, early, near),
        "own_first",
        unit,
        [first_shape] * near,
        [HBM] * 3,
        [pltpu.with_memory_space_constraint(one, pltpu.HBM) for one in (ids, key_vectors, value_vectors)],
        scratch_shapes=[
            pltpu.VMEM(ids.shape, ids.dtype),
            pltpu.VMEM((near, row_count, heads * width), key_vectors.dtype),
            pltpu.VMEM((near, row_count, max(early, 1) * width), value_vectors.dtype),
            pltpu.SemaphoreType.DMA((2 * near + 1,)),
        ],
    )
    own_rest = call(
        functools.partial(own_rest_kernel, width, heads, early),
        "own_rest",
        unit,
        [rest_shape] * near,
        [VMEM] * 3,
        (ids, key_vectors, value_vectors),
    )
    marked, marked_carries, states = [], [], []
    for own, shape in ((own_first, first_shape), (own_rest, rest_shape)):
        slots = exchange(own)
        block_total = call(
            functools.partial(total_kernel, mark_at, near),
            "block_total",
            unit // 4,
            shape,
            [VMEM] * (len(marked) + near),
            (*marked, *slots),
        )
        carries = onward(block_total)
        prefix = call(
            functools.partial(prefix_kernel, mark_at, near, steps),
            "prefixes",
            unit // 4,
            [shape] * near,
            [VMEM] * (len(marked) + len(marked_carries) + near + steps),
            (*marked, *marked_carries, *slots, *carries),
        )
        states.append(exchange(prefix))
        marked, marked_carries = marked or slots, marked_carries or carries
    count = near * early
    solved, local, out = call(
        functools.partial(solve_kernel, width, packs, early, max(1, 8 // heads)),
        "solve",
        12 * unit,
        [flat] * 3,
        [SMEM] + [VMEM] * (4 + near),
        (ridge_weight, ids, queries, key_vectors, value_vectors, *states[0]),
        out_specs=[VMEM, VMEM, HBM],
        scratch_shapes=[
            pltpu.VMEM((max(count, 1), row_count, width), jnp.float32),
            pltpu.SemaphoreType.DMA((max(count, 1),)),
        ],
    )
    count = near * (heads - early)
    return call(
        functools.partial(readout_kernel, width, heads, early, near),
        "readout",
        2 * unit,
        flat,
        [VMEM] * (2 + near) + [HBM],
        (solved, local, *states[1], out),
        out_specs=HBM,
        scratch_shapes=[pltpu.VMEM((count, row_count, width), jnp.float32), pltpu.SemaphoreType.DMA((count,))],
        input_output_aliases={2 + near: 0},
    )


def solution(mesh):
    outer, inner = mesh.shape["outer"], mesh.shape["inner"]
    finer = Mesh(mesh.devices.reshape(outer, 2, inner // 2), ("outer", "half", "near"))
    tokens = P(("outer", "half", "near"))
    return jax.shard_map(
        on_device, mesh=finer, in_specs=(tokens, tokens, tokens, tokens, P()), out_specs=tokens, check_vma=False
    )
```

```python
import functools

import jax
import jax.numpy as jnp
from jax import lax
from jax.experimental import pallas as pl
from jax.experimental.pallas import tpu as pltpu
from jax.sharding import Mesh
from jax.sharding import PartitionSpec as P

CG_ITERS = 3
DOC_SHARE = 4


def split(x):
    high = x.astype(jnp.bfloat16)
    low = (x - high.astype(jnp.float32)).astype(jnp.bfloat16)
    return high, low


def dot(a, b):
    return lax.dot_general(a, b, (((1,), (0,)), ((), ())), preferred_element_type=jnp.float32)


def dot_rows(a, b):
    return lax.dot_general(a, b, (((0,), (0,)), ((), ())), preferred_element_type=jnp.float32)


def total(terms):
    return functools.reduce(lambda a, b: a + b, terms)


def triangle(width):
    row = lax.broadcasted_iota(jnp.int32, (width, width), 0)
    col = lax.broadcasted_iota(jnp.int32, (width, width), 1)
    return row <= col, row == col


def down(ids):
    count = ids.shape[1]
    return jnp.broadcast_to(ids, (count, count)).T[:, :1]


def row_scale(wide):
    return lax.rsqrt(jnp.sum(wide * wide, -1, keepdims=True) + 1e-06)


def extra_of(packs):
    return -(-(packs + 2) // 8) * 8


def last_of(ids_ref, width):
    ids = ids_ref[...].astype(jnp.float32)
    oldest, newest = jnp.min(ids, 1, keepdims=True), jnp.max(ids, 1, keepdims=True)
    weight = jnp.broadcast_to((down(ids) == newest).astype(jnp.float32), (ids.shape[1], width))
    return oldest, newest, weight


def own_first_kernel(width, packs, early, masks, ids_hbm, k_hbm, v_hbm, *refs):
    count = len(masks)
    outs, (ids_ref, k_ref, v_ref, sems) = refs[:count], refs[count:]
    span = 2 * packs * width
    moves = [(ids_hbm, ids_ref)]
    for slot in range(count):
        start = pl.multiple_of((lax.axis_index("near") ^ masks[slot]) * span, span)
        moves.append((k_hbm.at[:, pl.ds(start, span)], k_ref.at[slot]))
        if early:
            moves.append((v_hbm.at[:, pl.ds(start, early * width)], v_ref.at[slot]))
    copies = [pltpu.make_async_copy(*move, sems.at[number]) for number, move in enumerate(moves)]
    for copy in copies:
        copy.start()
    upper, diagonal = triangle(width)
    for copy in copies:
        copy.wait()
    oldest, newest, weight = last_of(ids_ref, width)
    marks = [jnp.broadcast_to(one + 1.0, (1, width)) for one in (oldest, newest)]
    extra = extra_of(packs)
    filler = jnp.zeros((extra - packs - 2, width), jnp.float32)
    for slot, out in enumerate(outs):
        grams = []
        for head in range(2 * packs):
            lanes = pl.ds(head * width, width)
            keys = k_ref[slot, :, lanes]
            wide = keys.astype(jnp.float32)
            scale = row_scale(wide)
            light = weight * scale
            high, low = split(light * scale * wide)
            if head < early:
                v_high, v_low = split(light * v_ref[slot, :, lanes].astype(jnp.float32))
                high, low = jnp.concatenate([high, v_high], 1), jnp.concatenate([low, v_low], 1)
            both = dot_rows(jnp.concatenate([keys, keys], 0), jnp.concatenate([high, low], 0))
            grams.append(both[:, :width])
            if head < early:
                out[pl.ds((packs + head) * width + extra, width), :] = both[:, width:]
        seconds = []
        for pack in range(packs):
            one, two = grams[2 * pack : 2 * pack + 2]
            out[pl.ds(pack * width, width), :] = jnp.where(upper, one, two)
            seconds.append(jnp.sum(jnp.where(diagonal, two, 0.0), 0, keepdims=True))
        out[pl.ds(packs * width, extra), :] = jnp.concatenate([*seconds, *marks, filler], 0)


def own_rest_kernel(width, heads, early, masks, ids_ref, k_ref, v_ref, *outs):
    weight = last_of(ids_ref, width)[2]
    for slot, out in enumerate(outs):
        for head in range(early, heads):
            at = (lax.axis_index("near") ^ masks[slot]) * heads + head
            lanes = pl.ds(pl.multiple_of(at * width, width), width)
            keys = k_ref[:, lanes]
            scale = row_scale(keys.astype(jnp.float32))
            high, low = split(weight * scale * v_ref[:, lanes].astype(jnp.float32))
            out[pl.ds((head - early) * width, width), :] = dot_rows(
                jnp.concatenate([keys, keys], 0), jnp.concatenate([high, low], 0)
            )


def marks_of(refs, at):
    return [ref[pl.ds(at, 1), :] for ref in refs], [ref[pl.ds(at + 1, 1), :] for ref in refs]


def flag(condition):
    return condition.astype(jnp.float32)


def total_kernel(at, count, *refs):
    marked, slots, out = refs[:count], refs[-1 - count : -1], refs[-1]
    last = marks_of(marked, at)[1]
    newest = functools.reduce(jnp.maximum, last)
    out[...] = total([slot[...] * flag(one == newest) for slot, one in zip(slots, last)])
    if len(refs) == count + 1:
        out[pl.ds(at, 2), :] = jnp.concatenate([newest, newest], 0)


def prefix_kernel(at, steps, masks, out_masks, *refs):
    count = len(masks)
    outs, refs = refs[-count:], refs[:-count]
    marked, marked_carries = refs[:count], refs[count : count + steps]
    slots, carries = refs[-count - steps : -steps], refs[-steps:]
    first, last = marks_of(marked, at)
    oldest = functools.reduce(jnp.minimum, first)
    ends = marks_of(marked_carries, at)[1]
    carry = total([one[...] * flag(mark == oldest) for one, mark in zip(carries, ends)])
    me = lax.axis_index("near")
    for mask, out in zip(out_masks, outs):
        target = masks.index(mask)
        terms = [carry * flag(first[target] == oldest)]
        for source in range(count):
            if source != target:
                before = jnp.where((me ^ masks[source]) < (me ^ mask), 1.0, 0.0)
                terms.append(slots[source][...] * (flag(last[source] == first[target]) * before))
        out[...] = total(terms)


def far_part(pair, high, cross):
    c_high, c_low = split(cross)
    return dot(pair, jnp.concatenate([c_high, c_high], 0)) + dot(high, c_low)


def solve_kernel(width, packs, early, together, masks, ridge_ref, ids_ref, q_ref, k_ref, v_ref, *refs):
    slots, (x_ref, near_ref, out_hbm, out, sems) = refs[:-5], refs[-5:]
    upper, diagonal = triangle(width)
    ids = ids_ref[...].astype(jnp.float32)
    column = down(ids)
    rows = ids.shape[1]
    carried = jnp.broadcast_to(flag(column == jnp.min(ids, 1, keepdims=True)), (rows, width))
    row_at = lax.broadcasted_iota(jnp.int32, (rows, rows), 0)
    col_at = lax.broadcasted_iota(jnp.int32, (rows, rows), 1)
    within = jnp.where(row_at >= col_at, flag(column == ids), 0.0)
    copies = []
    for start in range(0, len(slots), together):
        group = []
        for slot, pack in [(j, p) for j in range(start, min(start + together, len(slots))) for p in range(packs)]:
            state = slots[slot]
            packed = state[pl.ds(pack * width, width), :]
            flipped = packed.T
            second = state[pl.ds(packs * width + pack, 1), :]
            grams = [
                jnp.where(upper, packed, flipped),
                jnp.where(diagonal, second, jnp.where(upper, flipped, packed)),
            ]
            for side in range(2):
                head = ((lax.axis_index("near") ^ masks[slot]) * packs + pack) * 2 + side
                lanes = pl.ds(pl.multiple_of(head * width, width), width)
                wide = q_ref[:, lanes].astype(jnp.float32)
                query = wide * row_scale(wide)
                keys = k_ref[:, lanes]
                turned = keys.astype(jnp.float32).T
                scale = lax.rsqrt(jnp.sum(turned * turned, 0, keepdims=True) + 1e-06)
                turned = turned.astype(jnp.bfloat16)
                high, low = split(grams[side])
                both = jnp.concatenate([high, turned], 1)
                group.append(
                    dict(
                        lanes=lanes,
                        cross=state.at[pl.ds((packs + 2 * pack + side) * width + extra_of(packs), width)]
                        if 2 * pack + side < early
                        else None,
                        both=jnp.concatenate([both, both], 0),
                        low=low,
                        turned=jnp.concatenate([turned, turned], 0),
                        keys=jnp.concatenate([keys, keys], 0),
                        once=within * scale,
                        twice=within * (scale * scale),
                        ridge=ridge_ref[head],
                        remain=query,
                        search=query,
                        square=jnp.sum(query * query, -1, keepdims=True),
                    )
                )
        for step in range(CG_ITERS):
            for h in group:
                high, low = split(h["search"])
                wide = dot(jnp.concatenate([high, low], 1), h["both"])
                h["state"] = wide[:, :width] + dot(high, h["low"])
                h["score"] = split(wide[:, width:] * h["twice"])
            for h in group:
                local = dot(jnp.concatenate(h["score"], 1), h["keys"])
                search = h["search"]
                applied = h["state"] * carried + local + h["ridge"] * search
                size = h["square"] / jnp.sum(search * applied, -1, keepdims=True)
                h["solved"] = size * search if step == 0 else h["solved"] + size * search
                if step < CG_ITERS - 1:
                    remain = h["remain"] - size * applied
                    square = jnp.sum(remain * remain, -1, keepdims=True)
                    h["search"] = remain + square / h["square"] * search
                    h["remain"], h["square"] = remain, square
        for h in group:
            high, low = split(h["solved"])
            pair = jnp.concatenate([high, low], 1)
            h["score"] = split(dot(pair, h["turned"]) * h["once"])
            if h["cross"] is None:
                x_ref[:, h["lanes"]] = h["solved"] * carried
            else:
                h["far"] = far_part(pair, high, h["cross"][...]) * carried
        for h in group:
            values = v_ref[:, h["lanes"]]
            local = dot(jnp.concatenate(h["score"], 1), jnp.concatenate([values, values], 0))
            if h["cross"] is None:
                near_ref[:, h["lanes"]] = local
            else:
                at = len(copies)
                out[at] = local + h["far"]
                copies.append(pltpu.make_async_copy(out.at[at], out_hbm.at[:, h["lanes"]], sems.at[at]))
                copies[-1].start()
    for copy in copies:
        copy.wait()


def readout_kernel(width, heads, early, masks, x_ref, near_ref, *refs):
    slots, (out_hbm, out, sems) = refs[: len(masks)], refs[-3:]
    copies = []
    for slot, state in enumerate(slots):
        for head in range(early, heads):
            at = (lax.axis_index("near") ^ masks[slot]) * heads + head
            lanes = pl.ds(pl.multiple_of(at * width, width), width)
            high, low = split(x_ref[:, lanes])
            far = far_part(jnp.concatenate([high, low], 1), high, state[pl.ds((head - early) * width, width), :])
            number = len(copies)
            out[number] = near_ref[:, lanes] + far
            copies.append(pltpu.make_async_copy(out.at[number], out_hbm.at[:, lanes], sems.at[number]))
            copies[-1].start()
    for copy in copies:
        copy.wait()


VMEM = pl.BlockSpec(memory_space=pltpu.VMEM)
SMEM = pl.BlockSpec(memory_space=pltpu.SMEM)
HBM = pl.BlockSpec(memory_space=pltpu.HBM)
PARAMS = pltpu.CompilerParams(vmem_limit_bytes=40 * 1024 * 1024)


def call(kernel, name, flops, out_shape, in_specs, arguments, **more):
    out_specs = [VMEM] * len(out_shape) if isinstance(out_shape, list) else VMEM
    return pl.pallas_call(
        kernel,
        out_shape=out_shape,
        in_specs=in_specs,
        compiler_params=PARAMS,
        cost_estimate=pl.CostEstimate(flops=flops, bytes_accessed=0, transcendentals=0),
        name=name,
        **{"out_specs": out_specs, **more},
    )(*arguments)


def on_device(queries, key_vectors, value_vectors, segment_ids, ridge_weight):
    row_count, columns = queries.shape
    head_count = ridge_weight.shape[0]
    width = columns // head_count
    outer, half, near = lax.axis_size("outer"), lax.axis_size("half"), lax.axis_size("near")
    blocks = outer * half
    heads = head_count // near
    packs = heads // 2
    early = heads // 4
    steps = min(-(-(row_count * near * blocks // DOC_SHARE - 1) // (row_count * near)), blocks - 1)
    ids = segment_ids.reshape(1, row_count)
    mark_at = packs * width + packs
    first_shape = jax.ShapeDtypeStruct(((packs + early) * width + extra_of(packs), width), jnp.float32)
    rest_shape = jax.ShapeDtypeStruct(((heads - early) * width, width), jnp.float32)
    flat = jax.ShapeDtypeStruct((row_count, columns), jnp.float32)
    unit = 16 * head_count * width * width * row_count

    def exchange(slots, masks):
        return [
            lax.ppermute(slot, "near", [(i, i ^ mask) for i in range(near)]) if mask else slot
            for slot, mask in zip(slots, masks)
        ]

    def onward(value):
        return [
            lax.ppermute(value, ("outer", "half"), [(i, (i + step) % blocks) for i in range(blocks)])
            for step in range(1, steps + 1)
        ]

    rising = list(range(near))
    falling = rising[:1] + rising[:0:-1]
    orders = falling, rising, falling, rising
    own_first = call(
        functools.partial(own_first_kernel, width, packs, early, orders[0]),
        "own_first",
        unit,
        [first_shape] * near,
        [HBM] * 3,
        [pltpu.with_memory_space_constraint(one, pltpu.HBM) for one in (ids, key_vectors, value_vectors)],
        scratch_shapes=[
            pltpu.VMEM(ids.shape, ids.dtype),
            pltpu.VMEM((near, row_count, heads * width), key_vectors.dtype),
            pltpu.VMEM((near, row_count, max(early, 1) * width), value_vectors.dtype),
            pltpu.SemaphoreType.DMA((2 * near + 1,)),
        ],
    )
    own_rest = call(
        functools.partial(own_rest_kernel, width, heads, early, orders[1]),
        "own_rest",
        unit,
        [rest_shape] * near,
        [VMEM] * 3,
        (ids, key_vectors, value_vectors),
    )
    marked, marked_carries, states = [], [], []
    for piece, (own, shape) in enumerate(((own_first, first_shape), (own_rest, rest_shape))):
        masks, out_masks = orders[piece], orders[2 + piece]
        slots = exchange(own, masks)
        if marked:
            marked = [marked[orders[0].index(mask)] for mask in masks]
        block_total = call(
            functools.partial(total_kernel, mark_at, near),
            "block_total",
            unit // 4,
            shape,
            [VMEM] * (len(marked) + near),
            (*marked, *slots),
        )
        carries = onward(block_total)
        prefix = call(
            functools.partial(prefix_kernel, mark_at, steps, masks, out_masks),
            "prefixes",
            unit // 4,
            [shape] * near,
            [VMEM] * (len(marked) + len(marked_carries) + near + steps),
            (*marked, *marked_carries, *slots, *carries),
        )
        states.append(exchange(prefix, out_masks))
        marked, marked_carries = marked or slots, marked_carries or carries
    count = near * early
    solved, local, out = call(
        functools.partial(solve_kernel, width, packs, early, max(1, 8 // heads), orders[2]),
        "solve",
        12 * unit,
        [flat] * 3,
        [SMEM] + [VMEM] * (4 + near),
        (ridge_weight, ids, queries, key_vectors, value_vectors, *states[0]),
        out_specs=[VMEM, VMEM, HBM],
        scratch_shapes=[
            pltpu.VMEM((max(count, 1), row_count, width), jnp.float32),
            pltpu.SemaphoreType.DMA((max(count, 1),)),
        ],
    )
    count = near * (heads - early)
    return call(
        functools.partial(readout_kernel, width, heads, early, orders[3]),
        "readout",
        2 * unit,
        flat,
        [VMEM] * (2 + near) + [HBM],
        (solved, local, *states[1], out),
        out_specs=HBM,
        scratch_shapes=[pltpu.VMEM((count, row_count, width), jnp.float32), pltpu.SemaphoreType.DMA((count,))],
        input_output_aliases={2 + near: 0},
    )


def solution(mesh):
    outer, inner = mesh.shape["outer"], mesh.shape["inner"]
    finer = Mesh(mesh.devices.reshape(outer, 2, inner // 2), ("outer", "half", "near"))
    tokens = P(("outer", "half", "near"))
    return jax.shard_map(
        on_device, mesh=finer, in_specs=(tokens, tokens, tokens, tokens, P()), out_specs=tokens, check_vma=False
    )
```

```python
import functools

import jax
import jax.numpy as jnp
from jax import lax
from jax.experimental import pallas as pl
from jax.experimental.pallas import tpu as pltpu
from jax.sharding import Mesh
from jax.sharding import PartitionSpec as P

CG_ITERS = 3
DOC_SHARE = 4


def split(x):
    high = x.astype(jnp.bfloat16)
    low = (x - high.astype(jnp.float32)).astype(jnp.bfloat16)
    return high, low


def dot(a, b):
    return lax.dot_general(a, b, (((1,), (0,)), ((), ())), preferred_element_type=jnp.float32)


def dot_rows(a, b):
    return lax.dot_general(a, b, (((0,), (0,)), ((), ())), preferred_element_type=jnp.float32)


def total(terms):
    return functools.reduce(lambda a, b: a + b, terms)


def triangle(width):
    row = lax.broadcasted_iota(jnp.int32, (width, width), 0)
    col = lax.broadcasted_iota(jnp.int32, (width, width), 1)
    return row <= col, row == col


def down(ids):
    count = ids.shape[1]
    return jnp.broadcast_to(ids, (count, count)).T[:, :1]


def row_scale(wide):
    return lax.rsqrt(jnp.sum(wide * wide, -1, keepdims=True) + 1e-06)


def extra_of(packs):
    return -(-(packs + 2) // 8) * 8


def last_of(ids_ref, width):
    ids = ids_ref[...].astype(jnp.float32)
    oldest, newest = jnp.min(ids, 1, keepdims=True), jnp.max(ids, 1, keepdims=True)
    weight = jnp.broadcast_to((down(ids) == newest).astype(jnp.float32), (ids.shape[1], width))
    return oldest, newest, weight


def first_slot(width, packs, early, out, keys_of, values_of, last):
    oldest, newest, weight = last
    upper, diagonal = triangle(width)
    extra = extra_of(packs)
    marks = [jnp.broadcast_to(one + 1.0, (1, width)) for one in (oldest, newest)]
    filler = jnp.zeros((extra - packs - 2, width), jnp.float32)
    grams = []
    for head in range(2 * packs):
        keys = keys_of(head)
        wide = keys.astype(jnp.float32)
        scale = row_scale(wide)
        light = weight * scale
        high, low = split(light * scale * wide)
        if head < early:
            v_high, v_low = split(light * values_of(head).astype(jnp.float32))
            high, low = jnp.concatenate([high, v_high], 1), jnp.concatenate([low, v_low], 1)
        both = dot_rows(jnp.concatenate([keys, keys], 0), jnp.concatenate([high, low], 0))
        grams.append(both[:, :width])
        if head < early:
            out[pl.ds((packs + head) * width + extra, width), :] = both[:, width:]
    seconds = []
    for pack in range(packs):
        one, two = grams[2 * pack : 2 * pack + 2]
        out[pl.ds(pack * width, width), :] = jnp.where(upper, one, two)
        seconds.append(jnp.sum(jnp.where(diagonal, two, 0.0), 0, keepdims=True))
    out[pl.ds(packs * width, extra), :] = jnp.concatenate([*seconds, *marks, filler], 0)


def own_first_kernel(width, packs, early, masks, ids_hbm, k_hbm, v_hbm, *refs):
    outs, (ids_ref, k_ref, v_ref, sems) = refs[: len(masks)], refs[len(masks) :]
    span = 2 * packs * width
    moves = [(ids_hbm, ids_ref)]
    for slot, mask in enumerate(masks):
        start = pl.multiple_of((lax.axis_index("near") ^ mask) * span, span)
        moves.append((k_hbm.at[:, pl.ds(start, span)], k_ref.at[slot]))
        if early:
            moves.append((v_hbm.at[:, pl.ds(start, early * width)], v_ref.at[slot]))
    copies = [pltpu.make_async_copy(*move, sems.at[number]) for number, move in enumerate(moves)]
    for copy in copies:
        copy.start()
    for copy in copies:
        copy.wait()
    last = last_of(ids_ref, width)
    for slot, out in enumerate(outs):
        keys_of, values_of = (lambda head, ref=ref: ref[slot, :, pl.ds(head * width, width)] for ref in (k_ref, v_ref))
        first_slot(width, packs, early, out, keys_of, values_of, last)


def own_rest_kernel(width, packs, early, masks, ids_ref, k_ref, v_ref, *outs):
    last = last_of(ids_ref, width)

    def lanes_of(mask, head):
        at = (lax.axis_index("near") ^ mask) * 2 * packs + head
        return pl.ds(pl.multiple_of(at * width, width), width)

    for mask, out in zip(masks, outs):
        for head in range(early, 2 * packs):
            lanes = lanes_of(mask, head)
            keys = k_ref[:, lanes]
            scale = row_scale(keys.astype(jnp.float32))
            high, low = split(last[2] * scale * v_ref[:, lanes].astype(jnp.float32))
            out[pl.ds((head - early) * width, width), :] = dot_rows(
                jnp.concatenate([keys, keys], 0), jnp.concatenate([high, low], 0)
            )
    keys_of, values_of = (lambda head, ref=ref: ref[:, lanes_of(0, head)] for ref in (k_ref, v_ref))
    first_slot(width, packs, early, outs[-1], keys_of, values_of, last)


def marks_of(refs, at):
    return [ref[pl.ds(at, 1), :] for ref in refs], [ref[pl.ds(at + 1, 1), :] for ref in refs]


def flag(condition):
    return condition.astype(jnp.float32)


def total_kernel(at, count, *refs):
    marked, slots, out = refs[:count], refs[-1 - count : -1], refs[-1]
    last = marks_of(marked, at)[1]
    newest = functools.reduce(jnp.maximum, last)
    out[...] = total([slot[...] * flag(one == newest) for slot, one in zip(slots, last)])
    if len(refs) == count + 1:
        out[pl.ds(at, 2), :] = jnp.concatenate([newest, newest], 0)


def prefix_kernel(at, steps, masks, out_masks, *refs):
    count = len(masks)
    outs, refs = refs[-count:], refs[:-count]
    marked, marked_carries = refs[:count], refs[count : count + steps]
    slots, carries = refs[-count - steps : -steps], refs[-steps:]
    first, last = marks_of(marked, at)
    oldest = functools.reduce(jnp.minimum, first)
    ends = marks_of(marked_carries, at)[1]
    carry = total([one[...] * flag(mark == oldest) for one, mark in zip(carries, ends)])
    me = lax.axis_index("near")
    for mask, out in zip(out_masks, outs):
        target = masks.index(mask)
        terms = [carry * flag(first[target] == oldest)]
        for source in range(count):
            if source != target:
                before = jnp.where((me ^ masks[source]) < (me ^ mask), 1.0, 0.0)
                terms.append(slots[source][...] * (flag(last[source] == first[target]) * before))
        out[...] = total(terms)


def far_part(pair, high, cross):
    c_high, c_low = split(cross)
    return dot(pair, jnp.concatenate([c_high, c_high], 0)) + dot(high, c_low)


def solve_kernel(width, packs, early, together, masks, ridge_ref, ids_ref, q_ref, k_ref, v_ref, *refs):
    slots, (x_ref, near_ref, out_hbm, out, sems) = refs[:-5], refs[-5:]
    upper, diagonal = triangle(width)
    ids = ids_ref[...].astype(jnp.float32)
    column = down(ids)
    rows = ids.shape[1]
    carried = jnp.broadcast_to(flag(column == jnp.min(ids, 1, keepdims=True)), (rows, width))
    row_at = lax.broadcasted_iota(jnp.int32, (rows, rows), 0)
    col_at = lax.broadcasted_iota(jnp.int32, (rows, rows), 1)
    within = jnp.where(row_at >= col_at, flag(column == ids), 0.0)
    copies = []
    for start in range(0, len(slots), together):
        group = []
        for slot, pack in [(j, p) for j in range(start, min(start + together, len(slots))) for p in range(packs)]:
            state = slots[slot]
            packed = state[pl.ds(pack * width, width), :]
            flipped = packed.T
            second = state[pl.ds(packs * width + pack, 1), :]
            grams = [
                jnp.where(upper, packed, flipped),
                jnp.where(diagonal, second, jnp.where(upper, flipped, packed)),
            ]
            for side in range(2):
                head = ((lax.axis_index("near") ^ masks[slot]) * packs + pack) * 2 + side
                lanes = pl.ds(pl.multiple_of(head * width, width), width)
                wide = q_ref[:, lanes].astype(jnp.float32)
                query = wide * row_scale(wide)
                keys = k_ref[:, lanes]
                turned = keys.astype(jnp.float32).T
                scale = lax.rsqrt(jnp.sum(turned * turned, 0, keepdims=True) + 1e-06)
                turned = turned.astype(jnp.bfloat16)
                high, low = split(grams[side])
                both = jnp.concatenate([high, turned], 1)
                group.append(
                    dict(
                        lanes=lanes,
                        cross=state.at[pl.ds((packs + 2 * pack + side) * width + extra_of(packs), width)]
                        if 2 * pack + side < early
                        else None,
                        both=jnp.concatenate([both, both], 0),
                        low=low,
                        turned=jnp.concatenate([turned, turned], 0),
                        keys=jnp.concatenate([keys, keys], 0),
                        once=within * scale,
                        twice=within * (scale * scale),
                        ridge=ridge_ref[head],
                        remain=query,
                        search=query,
                        square=jnp.sum(query * query, -1, keepdims=True),
                    )
                )
        for step in range(CG_ITERS):
            for h in group:
                high, low = split(h["search"])
                wide = dot(jnp.concatenate([high, low], 1), h["both"])
                h["state"] = wide[:, :width] + dot(high, h["low"])
                h["score"] = split(wide[:, width:] * h["twice"])
            for h in group:
                local = dot(jnp.concatenate(h["score"], 1), h["keys"])
                search = h["search"]
                applied = h["state"] * carried + local + h["ridge"] * search
                size = h["square"] / jnp.sum(search * applied, -1, keepdims=True)
                h["solved"] = size * search if step == 0 else h["solved"] + size * search
                if step < CG_ITERS - 1:
                    remain = h["remain"] - size * applied
                    square = jnp.sum(remain * remain, -1, keepdims=True)
                    h["search"] = remain + square / h["square"] * search
                    h["remain"], h["square"] = remain, square
        for h in group:
            high, low = split(h["solved"])
            pair = jnp.concatenate([high, low], 1)
            h["score"] = split(dot(pair, h["turned"]) * h["once"])
            if h["cross"] is None:
                x_ref[:, h["lanes"]] = h["solved"] * carried
            else:
                h["far"] = far_part(pair, high, h["cross"][...]) * carried
        for h in group:
            values = v_ref[:, h["lanes"]]
            local = dot(jnp.concatenate(h["score"], 1), jnp.concatenate([values, values], 0))
            if h["cross"] is None:
                near_ref[:, h["lanes"]] = local
            else:
                at = len(copies)
                out[at] = local + h["far"]
                copies.append(pltpu.make_async_copy(out.at[at], out_hbm.at[:, h["lanes"]], sems.at[at]))
                copies[-1].start()
    for copy in copies:
        copy.wait()


def readout_kernel(width, heads, early, masks, x_ref, near_ref, *refs):
    slots, (out_hbm, out, sems) = refs[: len(masks)], refs[-3:]
    copies = []
    for slot, state in enumerate(slots):
        for head in range(early, heads):
            at = (lax.axis_index("near") ^ masks[slot]) * heads + head
            lanes = pl.ds(pl.multiple_of(at * width, width), width)
            high, low = split(x_ref[:, lanes])
            far = far_part(jnp.concatenate([high, low], 1), high, state[pl.ds((head - early) * width, width), :])
            number = len(copies)
            out[number] = near_ref[:, lanes] + far
            copies.append(pltpu.make_async_copy(out.at[number], out_hbm.at[:, lanes], sems.at[number]))
            copies[-1].start()
    for copy in copies:
        copy.wait()


VMEM = pl.BlockSpec(memory_space=pltpu.VMEM)
SMEM = pl.BlockSpec(memory_space=pltpu.SMEM)
HBM = pl.BlockSpec(memory_space=pltpu.HBM)
PARAMS = pltpu.CompilerParams(vmem_limit_bytes=40 * 1024 * 1024)


def call(kernel, name, flops, out_shape, in_specs, arguments, **more):
    out_specs = [VMEM] * len(out_shape) if isinstance(out_shape, list) else VMEM
    return pl.pallas_call(
        kernel,
        out_shape=out_shape,
        in_specs=in_specs,
        compiler_params=PARAMS,
        cost_estimate=pl.CostEstimate(flops=flops, bytes_accessed=0, transcendentals=0),
        name=name,
        **{"out_specs": out_specs, **more},
    )(*arguments)


def on_device(queries, key_vectors, value_vectors, segment_ids, ridge_weight):
    row_count, columns = queries.shape
    head_count = ridge_weight.shape[0]
    width = columns // head_count
    outer, half, near = lax.axis_size("outer"), lax.axis_size("half"), lax.axis_size("near")
    blocks = outer * half
    heads = head_count // near
    packs = heads // 2
    early = heads // 4
    steps = min(-(-(row_count * near * blocks // DOC_SHARE - 1) // (row_count * near)), blocks - 1)
    ids = segment_ids.reshape(1, row_count)
    mark_at = packs * width + packs
    first_shape = jax.ShapeDtypeStruct(((packs + early) * width + extra_of(packs), width), jnp.float32)
    rest_shape = jax.ShapeDtypeStruct(((heads - early) * width, width), jnp.float32)
    flat = jax.ShapeDtypeStruct((row_count, columns), jnp.float32)
    unit = 16 * head_count * width * width * row_count

    def exchange(slots, masks):
        return [
            lax.ppermute(slot, "near", [(i, i ^ mask) for i in range(near)]) if mask else slot
            for slot, mask in zip(slots, masks)
        ]

    def onward(value):
        return [
            lax.ppermute(value, ("outer", "half"), [(i, (i + step) % blocks) for i in range(blocks)])
            for step in range(1, steps + 1)
        ]

    rising = list(range(near))
    falling = rising[:1] + rising[:0:-1]
    orders = falling, rising, falling, rising
    own_away = call(
        functools.partial(own_first_kernel, width, packs, early, orders[0][1:]),
        "own_first",
        unit,
        [first_shape] * (near - 1),
        [HBM] * 3,
        [pltpu.with_memory_space_constraint(one, pltpu.HBM) for one in (ids, key_vectors, value_vectors)],
        scratch_shapes=[
            pltpu.VMEM(ids.shape, ids.dtype),
            pltpu.VMEM((near - 1, row_count, heads * width), key_vectors.dtype),
            pltpu.VMEM((near - 1, row_count, max(early, 1) * width), value_vectors.dtype),
            pltpu.SemaphoreType.DMA((2 * near - 1,)),
        ],
    )
    *own_rest, own_here = call(
        functools.partial(own_rest_kernel, width, packs, early, orders[1]),
        "own_rest",
        unit,
        [rest_shape] * near + [first_shape],
        [VMEM] * 3,
        (ids, key_vectors, value_vectors),
    )
    own_first = [own_here, *own_away]
    marked, marked_carries, states = [], [], []
    for piece, (own, shape) in enumerate(((own_first, first_shape), (own_rest, rest_shape))):
        masks, out_masks = orders[piece], orders[2 + piece]
        slots = exchange(own, masks)
        if marked:
            marked = [marked[orders[0].index(mask)] for mask in masks]
        block_total = call(
            functools.partial(total_kernel, mark_at, near),
            "block_total",
            unit // 4,
            shape,
            [VMEM] * (len(marked) + near),
            (*marked, *slots),
        )
        carries = onward(block_total)
        prefix = call(
            functools.partial(prefix_kernel, mark_at, steps, masks, out_masks),
            "prefixes",
            unit // 4,
            [shape] * near,
            [VMEM] * (len(marked) + len(marked_carries) + near + steps),
            (*marked, *marked_carries, *slots, *carries),
        )
        states.append(exchange(prefix, out_masks))
        marked, marked_carries = marked or slots, marked_carries or carries
    count = near * early
    solved, local, out = call(
        functools.partial(solve_kernel, width, packs, early, max(1, 8 // heads), orders[2]),
        "solve",
        12 * unit,
        [flat] * 3,
        [SMEM] + [VMEM] * (4 + near),
        (ridge_weight, ids, queries, key_vectors, value_vectors, *states[0]),
        out_specs=[VMEM, VMEM, HBM],
        scratch_shapes=[
            pltpu.VMEM((max(count, 1), row_count, width), jnp.float32),
            pltpu.SemaphoreType.DMA((max(count, 1),)),
        ],
    )
    for slots in (range(near // 2), range(near // 2, near)):
        count = len(slots) * (heads - early)
        out = call(
            functools.partial(readout_kernel, width, heads, early, [orders[3][slot] for slot in slots]),
            "readout",
            2 * unit * len(slots) // near,
            flat,
            [VMEM] * (2 + len(slots)) + [HBM],
            (solved, local, *[states[1][slot] for slot in slots], out),
            out_specs=HBM,
            scratch_shapes=[pltpu.VMEM((count, row_count, width), jnp.float32), pltpu.SemaphoreType.DMA((count,))],
            input_output_aliases={2 + len(slots): 0},
        )
    return out


def solution(mesh):
    outer, inner = mesh.shape["outer"], mesh.shape["inner"]
    finer = Mesh(mesh.devices.reshape(outer, 2, inner // 2), ("outer", "half", "near"))
    tokens = P(("outer", "half", "near"))
    return jax.shard_map(
        on_device, mesh=finer, in_specs=(tokens, tokens, tokens, tokens, P()), out_specs=tokens, check_vma=False
    )
```

```python
import functools

import jax
import jax.numpy as jnp
from jax import lax
from jax.experimental import pallas as pl
from jax.experimental.pallas import tpu as pltpu
from jax.sharding import Mesh
from jax.sharding import PartitionSpec as P

CG_ITERS = 3
DOC_SHARE = 4


def split(x):
    high = x.astype(jnp.bfloat16)
    low = (x - high.astype(jnp.float32)).astype(jnp.bfloat16)
    return high, low


def dot(a, b):
    return lax.dot_general(a, b, (((1,), (0,)), ((), ())), preferred_element_type=jnp.float32)


def dot_rows(a, b):
    return lax.dot_general(a, b, (((0,), (0,)), ((), ())), preferred_element_type=jnp.float32)


def total(terms):
    return functools.reduce(lambda a, b: a + b, terms)


def triangle(width):
    row = lax.broadcasted_iota(jnp.int32, (width, width), 0)
    col = lax.broadcasted_iota(jnp.int32, (width, width), 1)
    return row <= col, row == col


def down(ids):
    count = ids.shape[1]
    return jnp.broadcast_to(ids, (count, count)).T[:, :1]


def row_scale(wide):
    return lax.rsqrt(jnp.sum(wide * wide, -1, keepdims=True) + 1e-06)


def extra_of(packs):
    return -(-(packs + 2) // 8) * 8


def last_of(ids_ref, width):
    ids = ids_ref[...].astype(jnp.float32)
    oldest, newest = jnp.min(ids, 1, keepdims=True), jnp.max(ids, 1, keepdims=True)
    weight = jnp.broadcast_to((down(ids) == newest).astype(jnp.float32), (ids.shape[1], width))
    return oldest, newest, weight


def first_slot(width, packs, early, out, keys_of, values_of, last):
    oldest, newest, weight = last
    upper, diagonal = triangle(width)
    extra = extra_of(packs)
    marks = [jnp.broadcast_to(one + 1.0, (1, width)) for one in (oldest, newest)]
    filler = jnp.zeros((extra - packs - 2, width), jnp.float32)
    grams = []
    for head in range(2 * packs):
        keys = keys_of(head)
        wide = keys.astype(jnp.float32)
        scale = row_scale(wide)
        light = weight * scale
        high, low = split(light * scale * wide)
        if head < early:
            v_high, v_low = split(light * values_of(head).astype(jnp.float32))
            high, low = jnp.concatenate([high, v_high], 1), jnp.concatenate([low, v_low], 1)
        both = dot_rows(jnp.concatenate([keys, keys], 0), jnp.concatenate([high, low], 0))
        grams.append(both[:, :width])
        if head < early:
            out[pl.ds((packs + head) * width + extra, width), :] = both[:, width:]
    seconds = []
    for pack in range(packs):
        one, two = grams[2 * pack : 2 * pack + 2]
        out[pl.ds(pack * width, width), :] = jnp.where(upper, one, two)
        seconds.append(jnp.sum(jnp.where(diagonal, two, 0.0), 0, keepdims=True))
    out[pl.ds(packs * width, extra), :] = jnp.concatenate([*seconds, *marks, filler], 0)


def own_first_kernel(width, packs, early, masks, ids_hbm, k_hbm, v_hbm, *refs):
    outs, (ids_ref, k_ref, v_ref, sems) = refs[: len(masks)], refs[len(masks) :]
    span = 2 * packs * width
    moves = [(ids_hbm, ids_ref)]
    for slot, mask in enumerate(masks):
        start = pl.multiple_of((lax.axis_index("near") ^ mask) * span, span)
        moves.append((k_hbm.at[:, pl.ds(start, span)], k_ref.at[slot]))
        if early:
            moves.append((v_hbm.at[:, pl.ds(start, early * width)], v_ref.at[slot]))
    copies = [pltpu.make_async_copy(*move, sems.at[number]) for number, move in enumerate(moves)]
    for copy in copies:
        copy.start()
    for copy in copies:
        copy.wait()
    last = last_of(ids_ref, width)
    for slot, out in enumerate(outs):
        keys_of, values_of = (lambda head, ref=ref: ref[slot, :, pl.ds(head * width, width)] for ref in (k_ref, v_ref))
        first_slot(width, packs, early, out, keys_of, values_of, last)


def own_rest_kernel(width, packs, early, later, masks, ids_ref, k_ref, v_ref, *outs):
    last = last_of(ids_ref, width)

    def lanes_of(mask, head):
        at = (lax.axis_index("near") ^ mask) * 2 * packs + head
        return pl.ds(pl.multiple_of(at * width, width), width)

    for mask, out in zip(masks, outs):
        for head in range(early, 2 * packs):
            lanes = lanes_of(mask, head)
            keys = k_ref[:, lanes]
            scale = row_scale(keys.astype(jnp.float32))
            high, low = split(last[2] * scale * v_ref[:, lanes].astype(jnp.float32))
            out[pl.ds((head - early) * width, width), :] = dot_rows(
                jnp.concatenate([keys, keys], 0), jnp.concatenate([high, low], 0)
            )
    for mask, out in zip(later, outs[len(masks) :]):
        keys_of, values_of = (lambda head, r=ref, m=mask: r[:, lanes_of(m, head)] for ref in (k_ref, v_ref))
        first_slot(width, packs, early, out, keys_of, values_of, last)


def marks_of(refs, at):
    return [ref[pl.ds(at, 1), :] for ref in refs], [ref[pl.ds(at + 1, 1), :] for ref in refs]


def flag(condition):
    return condition.astype(jnp.float32)


def total_kernel(at, count, *refs):
    marked, slots, out = refs[:count], refs[-1 - count : -1], refs[-1]
    last = marks_of(marked, at)[1]
    newest = functools.reduce(jnp.maximum, last)
    out[...] = total([slot[...] * flag(one == newest) for slot, one in zip(slots, last)])
    if len(refs) == count + 1:
        out[pl.ds(at, 2), :] = jnp.concatenate([newest, newest], 0)


def prefix_kernel(at, steps, masks, out_masks, *refs):
    count = len(masks)
    outs, refs = refs[-count:], refs[:-count]
    marked, marked_carries = refs[:count], refs[count : count + steps]
    slots, carries = refs[-count - steps : -steps], refs[-steps:]
    first, last = marks_of(marked, at)
    oldest = functools.reduce(jnp.minimum, first)
    ends = marks_of(marked_carries, at)[1]
    carry = total([one[...] * flag(mark == oldest) for one, mark in zip(carries, ends)])
    me = lax.axis_index("near")
    for mask, out in zip(out_masks, outs):
        target = masks.index(mask)
        terms = [carry * flag(first[target] == oldest)]
        for source in range(count):
            if source != target:
                before = jnp.where((me ^ masks[source]) < (me ^ mask), 1.0, 0.0)
                terms.append(slots[source][...] * (flag(last[source] == first[target]) * before))
        out[...] = total(terms)


def far_part(pair, high, cross):
    c_high, c_low = split(cross)
    return dot(pair, jnp.concatenate([c_high, c_high], 0)) + dot(high, c_low)


def solve_kernel(width, packs, early, together, masks, ridge_ref, ids_ref, q_ref, k_ref, v_ref, *refs):
    slots, (x_ref, near_ref, out_hbm, out, sems) = refs[:-5], refs[-5:]
    upper, diagonal = triangle(width)
    ids = ids_ref[...].astype(jnp.float32)
    column = down(ids)
    rows = ids.shape[1]
    carried = jnp.broadcast_to(flag(column == jnp.min(ids, 1, keepdims=True)), (rows, width))
    carried_pair = jnp.concatenate([carried, carried], 1).astype(jnp.bfloat16)
    row_at = lax.broadcasted_iota(jnp.int32, (rows, rows), 0)
    col_at = lax.broadcasted_iota(jnp.int32, (rows, rows), 1)
    within = jnp.where(row_at >= col_at, flag(column == ids), 0.0)
    copies = []
    for start in range(0, len(slots), together):
        group = []
        for slot, pack in [(j, p) for j in range(start, min(start + together, len(slots))) for p in range(packs)]:
            state = slots[slot]
            packed = state[pl.ds(pack * width, width), :]
            flipped = packed.T
            second = state[pl.ds(packs * width + pack, 1), :]
            grams = [
                jnp.where(upper, packed, flipped),
                jnp.where(diagonal, second, jnp.where(upper, flipped, packed)),
            ]
            for side in range(2):
                head = ((lax.axis_index("near") ^ masks[slot]) * packs + pack) * 2 + side
                lanes = pl.ds(pl.multiple_of(head * width, width), width)
                wide = q_ref[:, lanes].astype(jnp.float32)
                query = wide * row_scale(wide)
                keys = k_ref[:, lanes]
                turned = keys.astype(jnp.float32).T
                scale = lax.rsqrt(jnp.sum(turned * turned, 0, keepdims=True) + 1e-06)
                turned = turned.astype(jnp.bfloat16)
                high, low = split(grams[side])
                both = jnp.concatenate([high, turned], 1)
                group.append(
                    dict(
                        lanes=lanes,
                        twin=pl.ds(pl.multiple_of(head * 2 * width, 2 * width), 2 * width),
                        cross=state.at[pl.ds((packs + 2 * pack + side) * width + extra_of(packs), width)]
                        if 2 * pack + side < early
                        else None,
                        both=jnp.concatenate([both, both], 0),
                        low=low,
                        turned=jnp.concatenate([turned, turned], 0),
                        keys=jnp.concatenate([keys, keys], 0),
                        once=within * scale,
                        twice=within * (scale * scale),
                        ridge=ridge_ref[head],
                        remain=query,
                        search=query,
                        square=jnp.sum(query * query, -1, keepdims=True),
                    )
                )
        for step in range(CG_ITERS):
            for h in group:
                high, low = split(h["search"])
                wide = dot(jnp.concatenate([high, low], 1), h["both"])
                h["state"] = wide[:, :width] + dot(high, h["low"])
                h["score"] = split(wide[:, width:] * h["twice"])
            for h in group:
                local = dot(jnp.concatenate(h["score"], 1), h["keys"])
                search = h["search"]
                applied = h["state"] * carried + local + h["ridge"] * search
                size = h["square"] / jnp.sum(search * applied, -1, keepdims=True)
                h["solved"] = size * search if step == 0 else h["solved"] + size * search
                if step < CG_ITERS - 1:
                    remain = h["remain"] - size * applied
                    square = jnp.sum(remain * remain, -1, keepdims=True)
                    h["search"] = remain + square / h["square"] * search
                    h["remain"], h["square"] = remain, square
        for h in group:
            high, low = split(h["solved"])
            pair = jnp.concatenate([high, low], 1)
            h["score"] = split(dot(pair, h["turned"]) * h["once"])
            if h["cross"] is None:
                x_ref[:, h["twin"]] = pair * carried_pair
            else:
                h["far"] = far_part(pair, high, h["cross"][...]) * carried
        for h in group:
            values = v_ref[:, h["lanes"]]
            local = dot(jnp.concatenate(h["score"], 1), jnp.concatenate([values, values], 0))
            if h["cross"] is None:
                near_ref[:, h["lanes"]] = local
            else:
                at = len(copies)
                out[at] = local + h["far"]
                copies.append(pltpu.make_async_copy(out.at[at], out_hbm.at[:, h["lanes"]], sems.at[at]))
                copies[-1].start()
    for copy in copies:
        copy.wait()


def readout_kernel(width, heads, early, masks, x_ref, near_ref, *refs):
    slots, (out_hbm, out, sems) = refs[: len(masks)], refs[-3:]
    copies = []
    for slot, state in enumerate(slots):
        for head in range(early, heads):
            at = (lax.axis_index("near") ^ masks[slot]) * heads + head
            lanes = pl.ds(pl.multiple_of(at * width, width), width)
            pair = x_ref[:, pl.ds(pl.multiple_of(at * 2 * width, 2 * width), 2 * width)]
            far = far_part(pair, pair[:, :width], state[pl.ds((head - early) * width, width), :])
            number = len(copies)
            out[number] = near_ref[:, lanes] + far
            copies.append(pltpu.make_async_copy(out.at[number], out_hbm.at[:, lanes], sems.at[number]))
            copies[-1].start()
    for copy in copies:
        copy.wait()


VMEM = pl.BlockSpec(memory_space=pltpu.VMEM)
SMEM = pl.BlockSpec(memory_space=pltpu.SMEM)
HBM = pl.BlockSpec(memory_space=pltpu.HBM)
PARAMS = pltpu.CompilerParams(vmem_limit_bytes=40 * 1024 * 1024)


def call(kernel, name, flops, out_shape, in_specs, arguments, **more):
    out_specs = [VMEM] * len(out_shape) if isinstance(out_shape, list) else VMEM
    return pl.pallas_call(
        kernel,
        out_shape=out_shape,
        in_specs=in_specs,
        compiler_params=PARAMS,
        cost_estimate=pl.CostEstimate(flops=flops, bytes_accessed=0, transcendentals=0),
        name=name,
        **{"out_specs": out_specs, **more},
    )(*arguments)


def on_device(queries, key_vectors, value_vectors, segment_ids, ridge_weight):
    row_count, columns = queries.shape
    head_count = ridge_weight.shape[0]
    width = columns // head_count
    outer, half, near = lax.axis_size("outer"), lax.axis_size("half"), lax.axis_size("near")
    blocks = outer * half
    heads = head_count // near
    packs = heads // 2
    early = heads // 4
    steps = min(-(-(row_count * near * blocks // DOC_SHARE - 1) // (row_count * near)), blocks - 1)
    ids = segment_ids.reshape(1, row_count)
    mark_at = packs * width + packs
    first_shape = jax.ShapeDtypeStruct(((packs + early) * width + extra_of(packs), width), jnp.float32)
    rest_shape = jax.ShapeDtypeStruct(((heads - early) * width, width), jnp.float32)
    flat = jax.ShapeDtypeStruct((row_count, columns), jnp.float32)
    unit = 16 * head_count * width * width * row_count

    def exchange(slots, masks):
        return [
            lax.ppermute(slot, "near", [(i, i ^ mask) for i in range(near)]) if mask else slot
            for slot, mask in zip(slots, masks)
        ]

    def onward(value):
        return [
            lax.ppermute(value, ("outer", "half"), [(i, (i + step) % blocks) for i in range(blocks)])
            for step in range(1, steps + 1)
        ]

    rising = list(range(near))
    falling = rising[:1] + rising[:0:-1]
    orders = falling, rising, falling, rising
    soon, later = orders[0][1 : 1 + near // 2], orders[0][1 + near // 2 :] + [0]
    own_soon = call(
        functools.partial(own_first_kernel, width, packs, early, soon),
        "own_first",
        unit,
        [first_shape] * len(soon),
        [HBM] * 3,
        [pltpu.with_memory_space_constraint(one, pltpu.HBM) for one in (ids, key_vectors, value_vectors)],
        scratch_shapes=[
            pltpu.VMEM(ids.shape, ids.dtype),
            pltpu.VMEM((len(soon), row_count, heads * width), key_vectors.dtype),
            pltpu.VMEM((len(soon), row_count, max(early, 1) * width), value_vectors.dtype),
            pltpu.SemaphoreType.DMA((2 * len(soon) + 1,)),
        ],
    )
    own_more = call(
        functools.partial(own_rest_kernel, width, packs, early, later, orders[1]),
        "own_rest",
        unit,
        [rest_shape] * near + [first_shape] * len(later),
        [VMEM] * 3,
        (ids, key_vectors, value_vectors),
    )
    own_rest, own_later = own_more[:near], own_more[near:]
    own_first = [own_later[-1], *own_soon, *own_later[:-1]]
    marked, marked_carries, states = [], [], []
    for piece, (own, shape) in enumerate(((own_first, first_shape), (own_rest, rest_shape))):
        masks, out_masks = orders[piece], orders[2 + piece]
        slots = exchange(own, masks)
        if marked:
            marked = [marked[orders[0].index(mask)] for mask in masks]
        block_total = call(
            functools.partial(total_kernel, mark_at, near),
            "block_total",
            unit // 4,
            shape,
            [VMEM] * (len(marked) + near),
            (*marked, *slots),
        )
        carries = onward(block_total)
        prefix = call(
            functools.partial(prefix_kernel, mark_at, steps, masks, out_masks),
            "prefixes",
            unit // 4,
            [shape] * near,
            [VMEM] * (len(marked) + len(marked_carries) + near + steps),
            (*marked, *marked_carries, *slots, *carries),
        )
        states.append(exchange(prefix, out_masks))
        marked, marked_carries = marked or slots, marked_carries or carries
    count = near * early
    solved, local, out = call(
        functools.partial(solve_kernel, width, packs, early, max(1, 8 // heads), orders[2]),
        "solve",
        12 * unit,
        [jax.ShapeDtypeStruct((row_count, 2 * columns), jnp.bfloat16), flat, flat],
        [SMEM] + [VMEM] * (4 + near),
        (ridge_weight, ids, queries, key_vectors, value_vectors, *states[0]),
        out_specs=[VMEM, VMEM, HBM],
        scratch_shapes=[
            pltpu.VMEM((max(count, 1), row_count, width), jnp.float32),
            pltpu.SemaphoreType.DMA((max(count, 1),)),
        ],
    )
    for slots in (range(near // 2), range(near // 2, near)):
        count = len(slots) * (heads - early)
        out = call(
            functools.partial(readout_kernel, width, heads, early, [orders[3][slot] for slot in slots]),
            "readout",
            2 * unit * len(slots) // near,
            flat,
            [VMEM] * (2 + len(slots)) + [HBM],
            (solved, local, *[states[1][slot] for slot in slots], out),
            out_specs=HBM,
            scratch_shapes=[pltpu.VMEM((count, row_count, width), jnp.float32), pltpu.SemaphoreType.DMA((count,))],
            input_output_aliases={2 + len(slots): 0},
        )
    return out


def solution(mesh):
    outer, inner = mesh.shape["outer"], mesh.shape["inner"]
    finer = Mesh(mesh.devices.reshape(outer, 2, inner // 2), ("outer", "half", "near"))
    tokens = P(("outer", "half", "near"))
    return jax.shard_map(
        on_device, mesh=finer, in_specs=(tokens, tokens, tokens, tokens, P()), out_specs=tokens, check_vma=False
    )
```

```python
import functools

import jax
import jax.numpy as jnp
from jax import lax
from jax.experimental import pallas as pl
from jax.experimental.pallas import tpu as pltpu
from jax.sharding import Mesh
from jax.sharding import PartitionSpec as P

CG_ITERS = 3
DOC_SHARE = 4


def split(x):
    high = x.astype(jnp.bfloat16)
    low = (x - high.astype(jnp.float32)).astype(jnp.bfloat16)
    return high, low


def dot(a, b):
    return lax.dot_general(a, b, (((1,), (0,)), ((), ())), preferred_element_type=jnp.float32)


def dot_rows(a, b):
    return lax.dot_general(a, b, (((0,), (0,)), ((), ())), preferred_element_type=jnp.float32)


def total(terms):
    return functools.reduce(lambda a, b: a + b, terms)


def triangle(width):
    row = lax.broadcasted_iota(jnp.int32, (width, width), 0)
    col = lax.broadcasted_iota(jnp.int32, (width, width), 1)
    return row <= col, row == col


def down(ids):
    count = ids.shape[1]
    return jnp.broadcast_to(ids, (count, count)).T[:, :1]


def row_scale(wide):
    return lax.rsqrt(jnp.sum(wide * wide, -1, keepdims=True) + 1e-06)


def extra_of(packs):
    return -(-(packs + 2) // 8) * 8


def last_of(ids_ref, width):
    ids = ids_ref[...].astype(jnp.float32)
    oldest, newest = jnp.min(ids, 1, keepdims=True), jnp.max(ids, 1, keepdims=True)
    weight = jnp.broadcast_to((down(ids) == newest).astype(jnp.float32), (ids.shape[1], width))
    return oldest, newest, weight


def first_slot(width, packs, early, out, keys_of, values_of, last):
    oldest, newest, weight = last
    upper, diagonal = triangle(width)
    extra = extra_of(packs)
    marks = [jnp.broadcast_to(one + 1.0, (1, width)) for one in (oldest, newest)]
    filler = jnp.zeros((extra - packs - 2, width), jnp.float32)
    grams = []
    for head in range(2 * packs):
        keys = keys_of(head)
        wide = keys.astype(jnp.float32)
        scale = row_scale(wide)
        light = weight * scale
        high, low = split(light * scale * wide)
        if head < early:
            v_high, v_low = split(light * values_of(head).astype(jnp.float32))
            high, low = jnp.concatenate([high, v_high], 1), jnp.concatenate([low, v_low], 1)
        both = dot_rows(jnp.concatenate([keys, keys], 0), jnp.concatenate([high, low], 0))
        grams.append(both[:, :width])
        if head < early:
            out[pl.ds((packs + head) * width + extra, width), :] = both[:, width:]
    seconds = []
    for pack in range(packs):
        one, two = grams[2 * pack : 2 * pack + 2]
        out[pl.ds(pack * width, width), :] = jnp.where(upper, one, two)
        seconds.append(jnp.sum(jnp.where(diagonal, two, 0.0), 0, keepdims=True))
    out[pl.ds(packs * width, extra), :] = jnp.concatenate([*seconds, *marks, filler], 0)


def own_first_kernel(width, packs, early, masks, ids_hbm, k_hbm, v_hbm, *refs):
    outs, (ids_ref, k_ref, v_ref, sems) = refs[: len(masks)], refs[len(masks) :]
    span = 2 * packs * width
    moves = [(ids_hbm, ids_ref)]
    for slot, mask in enumerate(masks):
        start = pl.multiple_of((lax.axis_index("near") ^ mask) * span, span)
        moves.append((k_hbm.at[:, pl.ds(start, span)], k_ref.at[slot]))
        if early:
            moves.append((v_hbm.at[:, pl.ds(start, early * width)], v_ref.at[slot]))
    copies = [pltpu.make_async_copy(*move, sems.at[number]) for number, move in enumerate(moves)]
    for copy in copies:
        copy.start()
    for copy in copies:
        copy.wait()
    last = last_of(ids_ref, width)
    for slot, out in enumerate(outs):
        keys_of, values_of = (lambda head, ref=ref: ref[slot, :, pl.ds(head * width, width)] for ref in (k_ref, v_ref))
        first_slot(width, packs, early, out, keys_of, values_of, last)


def own_rest_kernel(width, packs, early, later, masks, ids_ref, k_ref, v_ref, *outs):
    last = last_of(ids_ref, width)

    def lanes_of(mask, head):
        at = (lax.axis_index("near") ^ mask) * 2 * packs + head
        return pl.ds(pl.multiple_of(at * width, width), width)

    for mask, out in zip(masks, outs):
        for head in range(early, 2 * packs):
            lanes = lanes_of(mask, head)
            keys = k_ref[:, lanes]
            scale = row_scale(keys.astype(jnp.float32))
            high, low = split(last[2] * scale * v_ref[:, lanes].astype(jnp.float32))
            out[pl.ds((head - early) * width, width), :] = dot_rows(
                jnp.concatenate([keys, keys], 0), jnp.concatenate([high, low], 0)
            )
    for mask, out in zip(later, outs[len(masks) :]):
        keys_of, values_of = (lambda head, r=ref, m=mask: r[:, lanes_of(m, head)] for ref in (k_ref, v_ref))
        first_slot(width, packs, early, out, keys_of, values_of, last)


def marks_of(refs, at):
    return [ref[pl.ds(at, 1), :] for ref in refs], [ref[pl.ds(at + 1, 1), :] for ref in refs]


def flag(condition):
    return condition.astype(jnp.float32)


def total_kernel(at, count, *refs):
    marked, slots, out = refs[:count], refs[-1 - count : -1], refs[-1]
    last = marks_of(marked, at)[1]
    newest = functools.reduce(jnp.maximum, last)
    out[...] = total([slot[...] * flag(one == newest) for slot, one in zip(slots, last)])
    if len(refs) == count + 1:
        out[pl.ds(at, 2), :] = jnp.concatenate([newest, newest], 0)


def prefix_kernel(at, steps, masks, out_masks, *refs):
    count = len(masks)
    outs, refs = refs[-count:], refs[:-count]
    marked, marked_carries = refs[:count], refs[count : count + steps]
    slots, carries = refs[-count - steps : -steps], refs[-steps:]
    first, last = marks_of(marked, at)
    oldest = functools.reduce(jnp.minimum, first)
    ends = marks_of(marked_carries, at)[1]
    carry = total([one[...] * flag(mark == oldest) for one, mark in zip(carries, ends)])
    me = lax.axis_index("near")
    for mask, out in zip(out_masks, outs):
        target = masks.index(mask)
        terms = [carry * flag(first[target] == oldest)]
        for source in range(count):
            if source != target:
                before = jnp.where((me ^ masks[source]) < (me ^ mask), 1.0, 0.0)
                terms.append(slots[source][...] * (flag(last[source] == first[target]) * before))
        out[...] = total(terms)


def far_part(pair, high, cross):
    c_high, c_low = split(cross)
    return dot(pair, jnp.concatenate([c_high, c_high], 0)) + dot(high, c_low)


def solve_kernel(width, packs, early, together, masks, ridge_ref, ids_ref, q_ref, k_ref, v_ref, *refs):
    slots, (x_ref, near_ref, out_hbm, out, sems) = refs[:-5], refs[-5:]
    upper, diagonal = triangle(width)
    ids = ids_ref[...].astype(jnp.float32)
    column = down(ids)
    rows = ids.shape[1]
    carried = jnp.broadcast_to(flag(column == jnp.min(ids, 1, keepdims=True)), (rows, width))
    carried_pair = jnp.concatenate([carried, carried], 1).astype(jnp.bfloat16)
    row_at = lax.broadcasted_iota(jnp.int32, (rows, rows), 0)
    col_at = lax.broadcasted_iota(jnp.int32, (rows, rows), 1)
    within = jnp.where(row_at >= col_at, flag(column == ids), 0.0)
    copies = []
    for start in range(0, len(slots), together):
        group = []
        for slot, pack in [(j, p) for j in range(start, min(start + together, len(slots))) for p in range(packs)]:
            state = slots[slot]
            packed = state[pl.ds(pack * width, width), :]
            flipped = packed.T
            second = state[pl.ds(packs * width + pack, 1), :]
            grams = [
                jnp.where(upper, packed, flipped),
                jnp.where(diagonal, second, jnp.where(upper, flipped, packed)),
            ]
            for side in range(2):
                head = ((lax.axis_index("near") ^ masks[slot]) * packs + pack) * 2 + side
                lanes = pl.ds(pl.multiple_of(head * width, width), width)
                wide = q_ref[:, lanes].astype(jnp.float32)
                query = wide * row_scale(wide)
                keys = k_ref[:, lanes]
                turned = keys.astype(jnp.float32).T
                scale = lax.rsqrt(jnp.sum(turned * turned, 0, keepdims=True) + 1e-06)
                turned = turned.astype(jnp.bfloat16)
                high, low = split(grams[side])
                both = jnp.concatenate([high, turned], 1)
                group.append(
                    dict(
                        lanes=lanes,
                        twin=pl.ds(pl.multiple_of(head * 2 * width, 2 * width), 2 * width),
                        cross=state.at[pl.ds((packs + 2 * pack + side) * width + extra_of(packs), width)]
                        if 2 * pack + side < early
                        else None,
                        both=jnp.concatenate([both, both], 0),
                        low=low,
                        turned=jnp.concatenate([turned, turned], 0),
                        keys=jnp.concatenate([keys, keys], 0),
                        once=within * scale,
                        twice=within * (scale * scale),
                        ridge=ridge_ref[head],
                        remain=query,
                        search=query,
                        square=jnp.sum(query * query, -1, keepdims=True),
                    )
                )
        for step in range(CG_ITERS):
            for h in group:
                high, low = split(h["search"])
                wide = dot(jnp.concatenate([high, low], 1), h["both"])
                h["state"] = wide[:, :width] + dot(high, h["low"])
                h["score"] = split(wide[:, width:] * h["twice"])
            for h in group:
                local = dot(jnp.concatenate(h["score"], 1), h["keys"])
                search = h["search"]
                applied = h["state"] * carried + local + h["ridge"] * search
                size = h["square"] / jnp.sum(search * applied, -1, keepdims=True)
                h["solved"] = size * search if step == 0 else h["solved"] + size * search
                if step < CG_ITERS - 1:
                    remain = h["remain"] - size * applied
                    square = jnp.sum(remain * remain, -1, keepdims=True)
                    h["search"] = remain + square / h["square"] * search
                    h["remain"], h["square"] = remain, square
        for h in group:
            high, low = split(h["solved"])
            pair = jnp.concatenate([high, low], 1)
            h["score"] = split(dot(pair, h["turned"]) * h["once"])
            if h["cross"] is None:
                x_ref[:, h["twin"]] = pair * carried_pair
            else:
                h["far"] = far_part(pair, high, h["cross"][...]) * carried
        for h in group:
            values = v_ref[:, h["lanes"]]
            local = dot(jnp.concatenate(h["score"], 1), jnp.concatenate([values, values], 0))
            if h["cross"] is None:
                near_ref[:, h["lanes"]] = local
            else:
                at = len(copies)
                out[at] = local + h["far"]
                copies.append(pltpu.make_async_copy(out.at[at], out_hbm.at[:, h["lanes"]], sems.at[at]))
                copies[-1].start()
    for copy in copies:
        copy.wait()


def readout_kernel(width, heads, early, masks, x_ref, near_ref, *refs):
    slots, (out_hbm, out, sems) = refs[: len(masks)], refs[-3:]
    copies = []
    group = heads - early
    for slot, state in enumerate(slots):
        start = (lax.axis_index("near") ^ masks[slot]) * heads + early
        for head in range(group):
            at = start + head
            lanes = pl.ds(pl.multiple_of(at * width, width), width)
            pair = x_ref[:, pl.ds(pl.multiple_of(at * 2 * width, 2 * width), 2 * width)]
            far = far_part(pair, pair[:, :width], state[pl.ds(head * width, width), :])
            out[slot, :, pl.ds(head * width, width)] = near_ref[:, lanes] + far
        span = pl.ds(pl.multiple_of(start * width, width), group * width)
        copies.append(pltpu.make_async_copy(out.at[slot], out_hbm.at[:, span], sems.at[slot]))
        copies[-1].start()
    for copy in copies:
        copy.wait()


VMEM = pl.BlockSpec(memory_space=pltpu.VMEM)
SMEM = pl.BlockSpec(memory_space=pltpu.SMEM)
HBM = pl.BlockSpec(memory_space=pltpu.HBM)
PARAMS = pltpu.CompilerParams(vmem_limit_bytes=40 * 1024 * 1024)


def call(kernel, name, flops, out_shape, in_specs, arguments, **more):
    out_specs = [VMEM] * len(out_shape) if isinstance(out_shape, list) else VMEM
    return pl.pallas_call(
        kernel,
        out_shape=out_shape,
        in_specs=in_specs,
        compiler_params=PARAMS,
        cost_estimate=pl.CostEstimate(flops=flops, bytes_accessed=0, transcendentals=0),
        name=name,
        **{"out_specs": out_specs, **more},
    )(*arguments)


def on_device(queries, key_vectors, value_vectors, segment_ids, ridge_weight):
    row_count, columns = queries.shape
    head_count = ridge_weight.shape[0]
    width = columns // head_count
    outer, half, near = lax.axis_size("outer"), lax.axis_size("half"), lax.axis_size("near")
    blocks = outer * half
    heads = head_count // near
    packs = heads // 2
    early = heads // 4
    steps = min(-(-(row_count * near * blocks // DOC_SHARE - 1) // (row_count * near)), blocks - 1)
    ids = segment_ids.reshape(1, row_count)
    mark_at = packs * width + packs
    first_shape = jax.ShapeDtypeStruct(((packs + early) * width + extra_of(packs), width), jnp.float32)
    rest_shape = jax.ShapeDtypeStruct(((heads - early) * width, width), jnp.float32)
    flat = jax.ShapeDtypeStruct((row_count, columns), jnp.float32)
    unit = 16 * head_count * width * width * row_count

    def exchange(slots, masks):
        return [
            lax.ppermute(slot, "near", [(i, i ^ mask) for i in range(near)]) if mask else slot
            for slot, mask in zip(slots, masks)
        ]

    def onward(value):
        return [
            lax.ppermute(value, ("outer", "half"), [(i, (i + step) % blocks) for i in range(blocks)])
            for step in range(1, steps + 1)
        ]

    rising = list(range(near))
    falling = rising[:1] + rising[:0:-1]
    orders = falling, rising, falling, rising
    soon, later = orders[0][1 : 1 + near // 2], orders[0][1 + near // 2 :] + [0]
    own_soon = call(
        functools.partial(own_first_kernel, width, packs, early, soon),
        "own_first",
        unit,
        [first_shape] * len(soon),
        [HBM] * 3,
        [pltpu.with_memory_space_constraint(one, pltpu.HBM) for one in (ids, key_vectors, value_vectors)],
        scratch_shapes=[
            pltpu.VMEM(ids.shape, ids.dtype),
            pltpu.VMEM((len(soon), row_count, heads * width), key_vectors.dtype),
            pltpu.VMEM((len(soon), row_count, max(early, 1) * width), value_vectors.dtype),
            pltpu.SemaphoreType.DMA((2 * len(soon) + 1,)),
        ],
    )
    own_more = call(
        functools.partial(own_rest_kernel, width, packs, early, later, orders[1]),
        "own_rest",
        unit,
        [rest_shape] * near + [first_shape] * len(later),
        [VMEM] * 3,
        (ids, key_vectors, value_vectors),
    )
    own_rest, own_later = own_more[:near], own_more[near:]
    own_first = [own_later[-1], *own_soon, *own_later[:-1]]
    marked, marked_carries, states = [], [], []
    for piece, (own, shape) in enumerate(((own_first, first_shape), (own_rest, rest_shape))):
        masks, out_masks = orders[piece], orders[2 + piece]
        slots = exchange(own, masks)
        if marked:
            marked = [marked[orders[0].index(mask)] for mask in masks]
        block_total = call(
            functools.partial(total_kernel, mark_at, near),
            "block_total",
            unit // 4,
            shape,
            [VMEM] * (len(marked) + near),
            (*marked, *slots),
        )
        carries = onward(block_total)
        prefix = call(
            functools.partial(prefix_kernel, mark_at, steps, masks, out_masks),
            "prefixes",
            unit // 4,
            [shape] * near,
            [VMEM] * (len(marked) + len(marked_carries) + near + steps),
            (*marked, *marked_carries, *slots, *carries),
        )
        states.append(exchange(prefix, out_masks))
        marked, marked_carries = marked or slots, marked_carries or carries
    count = near * early
    solved, local, out = call(
        functools.partial(solve_kernel, width, packs, early, max(1, 8 // heads), orders[2]),
        "solve",
        12 * unit,
        [jax.ShapeDtypeStruct((row_count, 2 * columns), jnp.bfloat16), flat, flat],
        [SMEM] + [VMEM] * (4 + near),
        (ridge_weight, ids, queries, key_vectors, value_vectors, *states[0]),
        out_specs=[VMEM, VMEM, HBM],
        scratch_shapes=[
            pltpu.VMEM((max(count, 1), row_count, width), jnp.float32),
            pltpu.SemaphoreType.DMA((max(count, 1),)),
        ],
    )
    for slots in (range(near // 2), range(near // 2, near)):
        out = call(
            functools.partial(readout_kernel, width, heads, early, [orders[3][slot] for slot in slots]),
            "readout",
            2 * unit * len(slots) // near,
            flat,
            [VMEM] * (2 + len(slots)) + [HBM],
            (solved, local, *[states[1][slot] for slot in slots], out),
            out_specs=HBM,
            scratch_shapes=[
                pltpu.VMEM((len(slots), row_count, (heads - early) * width), jnp.float32),
                pltpu.SemaphoreType.DMA((len(slots),)),
            ],
            input_output_aliases={2 + len(slots): 0},
        )
    return out


def solution(mesh):
    outer, inner = mesh.shape["outer"], mesh.shape["inner"]
    finer = Mesh(mesh.devices.reshape(outer, 2, inner // 2), ("outer", "half", "near"))
    tokens = P(("outer", "half", "near"))
    return jax.shard_map(
        on_device, mesh=finer, in_specs=(tokens, tokens, tokens, tokens, P()), out_specs=tokens, check_vma=False
    )
```

```python
import functools

import jax
import jax.numpy as jnp
from jax import lax
from jax.experimental import pallas as pl
from jax.experimental.pallas import tpu as pltpu
from jax.sharding import Mesh
from jax.sharding import PartitionSpec as P

CG_ITERS = 3
DOC_SHARE = 4


def split(x):
    high = x.astype(jnp.bfloat16)
    low = (x - high.astype(jnp.float32)).astype(jnp.bfloat16)
    return high, low


def dot(a, b):
    return lax.dot_general(a, b, (((1,), (0,)), ((), ())), preferred_element_type=jnp.float32)


def dot_rows(a, b):
    return lax.dot_general(a, b, (((0,), (0,)), ((), ())), preferred_element_type=jnp.float32)


def total(terms):
    return functools.reduce(lambda a, b: a + b, terms)


def triangle(width):
    row = lax.broadcasted_iota(jnp.int32, (width, width), 0)
    col = lax.broadcasted_iota(jnp.int32, (width, width), 1)
    return row <= col, row == col


def down(ids):
    count = ids.shape[1]
    return jnp.broadcast_to(ids, (count, count)).T[:, :1]


def row_scale(wide):
    return lax.rsqrt(jnp.sum(wide * wide, -1, keepdims=True) + 1e-06)


def extra_of(packs):
    return -(-(packs + 2) // 8) * 8


def last_of(ids_ref, width):
    ids = ids_ref[...].astype(jnp.float32)
    oldest, newest = jnp.min(ids, 1, keepdims=True), jnp.max(ids, 1, keepdims=True)
    weight = jnp.broadcast_to((down(ids) == newest).astype(jnp.float32), (ids.shape[1], width))
    return oldest, newest, weight


def first_slot(width, packs, early, out, keys_of, values_of, last):
    oldest, newest, weight = last
    upper, diagonal = triangle(width)
    extra = extra_of(packs)
    marks = [jnp.broadcast_to(one + 1.0, (1, width)) for one in (oldest, newest)]
    filler = jnp.zeros((extra - packs - 2, width), jnp.float32)
    grams = []
    for head in range(2 * packs):
        keys = keys_of(head)
        wide = keys.astype(jnp.float32)
        scale = row_scale(wide)
        light = weight * scale
        high, low = split(light * scale * wide)
        if head < early:
            v_high, v_low = split(light * values_of(head).astype(jnp.float32))
            high, low = jnp.concatenate([high, v_high], 1), jnp.concatenate([low, v_low], 1)
        both = dot_rows(jnp.concatenate([keys, keys], 0), jnp.concatenate([high, low], 0))
        grams.append(both[:, :width])
        if head < early:
            out[pl.ds((packs + head) * width + extra, width), :] = both[:, width:]
    seconds = []
    for pack in range(packs):
        one, two = grams[2 * pack : 2 * pack + 2]
        out[pl.ds(pack * width, width), :] = jnp.where(upper, one, two)
        seconds.append(jnp.sum(jnp.where(diagonal, two, 0.0), 0, keepdims=True))
    out[pl.ds(packs * width, extra), :] = jnp.concatenate([*seconds, *marks, filler], 0)


def own_first_kernel(width, packs, early, masks, ids_hbm, k_hbm, v_hbm, *refs):
    outs, (ids_ref, k_ref, v_ref, sems) = refs[: len(masks)], refs[len(masks) :]
    span = 2 * packs * width
    moves = [(ids_hbm, ids_ref)]
    for slot, mask in enumerate(masks):
        start = pl.multiple_of((lax.axis_index("near") ^ mask) * span, span)
        moves.append((k_hbm.at[:, pl.ds(start, span)], k_ref.at[slot]))
        if early:
            moves.append((v_hbm.at[:, pl.ds(start, early * width)], v_ref.at[slot]))
    copies = [pltpu.make_async_copy(*move, sems.at[number]) for number, move in enumerate(moves)]
    for copy in copies:
        copy.start()
    for copy in copies:
        copy.wait()
    last = last_of(ids_ref, width)
    for slot, out in enumerate(outs):
        keys_of, values_of = (lambda head, ref=ref: ref[slot, :, pl.ds(head * width, width)] for ref in (k_ref, v_ref))
        first_slot(width, packs, early, out, keys_of, values_of, last)


def own_rest_kernel(width, packs, early, later, masks, ids_ref, k_ref, v_ref, *outs):
    last = last_of(ids_ref, width)

    def lanes_of(mask, head):
        at = (lax.axis_index("near") ^ mask) * 2 * packs + head
        return pl.ds(pl.multiple_of(at * width, width), width)

    for mask, out in zip(masks, outs):
        for head in range(early, 2 * packs):
            lanes = lanes_of(mask, head)
            keys = k_ref[:, lanes]
            scale = row_scale(keys.astype(jnp.float32))
            high, low = split(last[2] * scale * v_ref[:, lanes].astype(jnp.float32))
            out[pl.ds((head - early) * width, width), :] = dot_rows(
                jnp.concatenate([keys, keys], 0), jnp.concatenate([high, low], 0)
            )
    for mask, out in zip(later, outs[len(masks) :]):
        keys_of, values_of = (lambda head, r=ref, m=mask: r[:, lanes_of(m, head)] for ref in (k_ref, v_ref))
        first_slot(width, packs, early, out, keys_of, values_of, last)


def marks_of(refs, at):
    return [ref[pl.ds(at, 1), :] for ref in refs], [ref[pl.ds(at + 1, 1), :] for ref in refs]


def flag(condition):
    return condition.astype(jnp.float32)


def total_kernel(at, count, *refs):
    marked, slots, out = refs[:count], refs[-1 - count : -1], refs[-1]
    last = marks_of(marked, at)[1]
    newest = functools.reduce(jnp.maximum, last)
    out[...] = total([slot[...] * flag(one == newest) for slot, one in zip(slots, last)])
    if len(refs) == count + 1:
        out[pl.ds(at, 2), :] = jnp.concatenate([newest, newest], 0)


def prefix_kernel(at, steps, masks, out_masks, *refs):
    count = len(masks)
    outs, refs = refs[-count:], refs[:-count]
    marked, marked_carries = refs[:count], refs[count : count + steps]
    slots, carries = refs[-count - steps : -steps], refs[-steps:]
    first, last = marks_of(marked, at)
    oldest = functools.reduce(jnp.minimum, first)
    ends = marks_of(marked_carries, at)[1]
    carry = total([one[...] * flag(mark == oldest) for one, mark in zip(carries, ends)])
    me = lax.axis_index("near")
    for mask, out in zip(out_masks, outs):
        target = masks.index(mask)
        terms = [carry * flag(first[target] == oldest)]
        for source in range(count):
            if source != target:
                before = jnp.where((me ^ masks[source]) < (me ^ mask), 1.0, 0.0)
                terms.append(slots[source][...] * (flag(last[source] == first[target]) * before))
        out[...] = total(terms)


def far_part(pair, high, cross):
    c_high, c_low = split(cross)
    return dot(pair, jnp.concatenate([c_high, c_high], 0)) + dot(high, c_low)


def solve_kernel(width, packs, early, together, masks, ridge_ref, ids_ref, q_ref, k_ref, v_ref, *refs):
    slots, (x_ref, near_ref, out_hbm, out, sems) = refs[:-5], refs[-5:]
    upper, diagonal = triangle(width)
    ids = ids_ref[...].astype(jnp.float32)
    column = down(ids)
    rows = ids.shape[1]
    carried = jnp.broadcast_to(flag(column == jnp.min(ids, 1, keepdims=True)), (rows, width))
    carried_pair = jnp.concatenate([carried, carried], 1).astype(jnp.bfloat16)
    row_at = lax.broadcasted_iota(jnp.int32, (rows, rows), 0)
    col_at = lax.broadcasted_iota(jnp.int32, (rows, rows), 1)
    within = jnp.where(row_at >= col_at, flag(column == ids), 0.0)
    copies = []
    for start in range(0, len(slots), together):
        group = []
        for slot, pack in [(j, p) for j in range(start, min(start + together, len(slots))) for p in range(packs)]:
            state = slots[slot]
            packed = state[pl.ds(pack * width, width), :]
            flipped = packed.T
            second = state[pl.ds(packs * width + pack, 1), :]
            grams = [
                jnp.where(upper, packed, flipped),
                jnp.where(diagonal, second, jnp.where(upper, flipped, packed)),
            ]
            for side in range(2):
                head = ((lax.axis_index("near") ^ masks[slot]) * packs + pack) * 2 + side
                lanes = pl.ds(pl.multiple_of(head * width, width), width)
                wide = q_ref[:, lanes].astype(jnp.float32)
                query = wide * row_scale(wide)
                keys = k_ref[:, lanes]
                turned = keys.astype(jnp.float32).T
                scale = lax.rsqrt(jnp.sum(turned * turned, 0, keepdims=True) + 1e-06)
                turned = turned.astype(jnp.bfloat16)
                high, low = split(grams[side])
                both = jnp.concatenate([high, turned], 1)
                group.append(
                    dict(
                        lanes=lanes,
                        twin=pl.ds(pl.multiple_of(head * 2 * width, 2 * width), 2 * width),
                        cross=state.at[pl.ds((packs + 2 * pack + side) * width + extra_of(packs), width)]
                        if 2 * pack + side < early
                        else None,
                        both=jnp.concatenate([both, both], 0),
                        low=low,
                        turned=jnp.concatenate([turned, turned], 0),
                        keys=jnp.concatenate([keys, keys], 0),
                        once=within * scale,
                        twice=within * (scale * scale),
                        ridge=ridge_ref[head],
                        remain=query,
                        search=query,
                        square=jnp.sum(query * query, -1, keepdims=True),
                    )
                )
        for step in range(CG_ITERS):
            for h in group:
                high, low = split(h["search"])
                wide = dot(jnp.concatenate([high, low], 1), h["both"])
                h["state"] = wide[:, :width] + dot(high, h["low"])
                h["score"] = split(wide[:, width:] * h["twice"])
            for h in group:
                local = dot(jnp.concatenate(h["score"], 1), h["keys"])
                search = h["search"]
                applied = h["state"] * carried + local + h["ridge"] * search
                size = h["square"] / jnp.sum(search * applied, -1, keepdims=True)
                h["solved"] = size * search if step == 0 else h["solved"] + size * search
                if step < CG_ITERS - 1:
                    remain = h["remain"] - size * applied
                    square = jnp.sum(remain * remain, -1, keepdims=True)
                    h["search"] = remain + square / h["square"] * search
                    h["remain"], h["square"] = remain, square
        for h in group:
            high, low = split(h["solved"])
            pair = jnp.concatenate([high, low], 1)
            h["score"] = split(dot(pair, h["turned"]) * h["once"])
            if h["cross"] is None:
                x_ref[:, h["twin"]] = pair * carried_pair
            else:
                h["far"] = far_part(pair, high, h["cross"][...]) * carried
        for h in group:
            values = v_ref[:, h["lanes"]]
            local = dot(jnp.concatenate(h["score"], 1), jnp.concatenate([values, values], 0))
            if h["cross"] is None:
                near_ref[:, h["lanes"]] = local
            else:
                at = len(copies)
                out[at] = local + h["far"]
                copies.append(pltpu.make_async_copy(out.at[at], out_hbm.at[:, h["lanes"]], sems.at[at]))
                copies[-1].start()
    for copy in copies:
        copy.wait()


def readout_kernel(width, heads, early, masks, x_ref, near_ref, *refs):
    slots, (out_hbm, out, sems) = refs[: len(masks)], refs[-3:]
    copies = []
    group = heads - early
    for slot, state in enumerate(slots):
        start = (lax.axis_index("near") ^ masks[slot]) * heads + early
        for head in range(group):
            at = start + head
            lanes = pl.ds(pl.multiple_of(at * width, width), width)
            pair = x_ref[:, pl.ds(pl.multiple_of(at * 2 * width, 2 * width), 2 * width)]
            far = far_part(pair, pair[:, :width], state[pl.ds(head * width, width), :])
            out[slot, :, pl.ds(head * width, width)] = near_ref[:, lanes] + far
        span = pl.ds(pl.multiple_of(start * width, width), group * width)
        copies.append(pltpu.make_async_copy(out.at[slot], out_hbm.at[:, span], sems.at[slot]))
        copies[-1].start()
    for copy in copies:
        copy.wait()


VMEM = pl.BlockSpec(memory_space=pltpu.VMEM)
SMEM = pl.BlockSpec(memory_space=pltpu.SMEM)
HBM = pl.BlockSpec(memory_space=pltpu.HBM)
PARAMS = pltpu.CompilerParams(vmem_limit_bytes=40 * 1024 * 1024)


def call(kernel, name, flops, out_shape, in_specs, arguments, **more):
    out_specs = [VMEM] * len(out_shape) if isinstance(out_shape, list) else VMEM
    return pl.pallas_call(
        kernel,
        out_shape=out_shape,
        in_specs=in_specs,
        compiler_params=PARAMS,
        cost_estimate=pl.CostEstimate(flops=flops, bytes_accessed=0, transcendentals=0),
        name=name,
        **{"out_specs": out_specs, **more},
    )(*arguments)


def on_device(queries, key_vectors, value_vectors, segment_ids, ridge_weight):
    row_count, columns = queries.shape
    head_count = ridge_weight.shape[0]
    width = columns // head_count
    outer, half, near = lax.axis_size("outer"), lax.axis_size("half"), lax.axis_size("near")
    blocks = outer * half
    heads = head_count // near
    packs = heads // 2
    early = heads // 4
    steps = min(-(-(row_count * near * blocks // DOC_SHARE - 1) // (row_count * near)), blocks - 1)
    ids = segment_ids.reshape(1, row_count)
    mark_at = packs * width + packs
    first_shape = jax.ShapeDtypeStruct(((packs + early) * width + extra_of(packs), width), jnp.float32)
    rest_shape = jax.ShapeDtypeStruct(((heads - early) * width, width), jnp.float32)
    flat = jax.ShapeDtypeStruct((row_count, columns), jnp.float32)
    unit = 16 * head_count * width * width * row_count

    def exchange(slots, masks):
        return [
            lax.ppermute(slot, "near", [(i, i ^ mask) for i in range(near)]) if mask else slot
            for slot, mask in zip(slots, masks)
        ]

    def onward(value):
        return [
            lax.ppermute(value, ("outer", "half"), [(i, (i + step) % blocks) for i in range(blocks)])
            for step in range(1, steps + 1)
        ]

    rising = list(range(near))
    falling = rising[:1] + rising[:0:-1]
    orders = falling, rising, rising[:1] + rising[-1:] + rising[1:-1], rising
    soon, later = orders[0][1 : 1 + near // 2], orders[0][1 + near // 2 :] + [0]
    own_soon = call(
        functools.partial(own_first_kernel, width, packs, early, soon),
        "own_first",
        unit,
        [first_shape] * len(soon),
        [HBM] * 3,
        [pltpu.with_memory_space_constraint(one, pltpu.HBM) for one in (ids, key_vectors, value_vectors)],
        scratch_shapes=[
            pltpu.VMEM(ids.shape, ids.dtype),
            pltpu.VMEM((len(soon), row_count, heads * width), key_vectors.dtype),
            pltpu.VMEM((len(soon), row_count, max(early, 1) * width), value_vectors.dtype),
            pltpu.SemaphoreType.DMA((2 * len(soon) + 1,)),
        ],
    )
    own_more = call(
        functools.partial(own_rest_kernel, width, packs, early, later, orders[1]),
        "own_rest",
        unit,
        [rest_shape] * near + [first_shape] * len(later),
        [VMEM] * 3,
        (ids, key_vectors, value_vectors),
    )
    own_rest, own_later = own_more[:near], own_more[near:]
    own_first = [own_later[-1], *own_soon, *own_later[:-1]]
    marked, marked_carries, states = [], [], []
    for piece, (own, shape) in enumerate(((own_first, first_shape), (own_rest, rest_shape))):
        masks, out_masks = orders[piece], orders[2 + piece]
        slots = exchange(own, masks)
        if marked:
            marked = [marked[orders[0].index(mask)] for mask in masks]
        block_total = call(
            functools.partial(total_kernel, mark_at, near),
            "block_total",
            unit // 4,
            shape,
            [VMEM] * (len(marked) + near),
            (*marked, *slots),
        )
        carries = onward(block_total)
        prefix = call(
            functools.partial(prefix_kernel, mark_at, steps, masks, out_masks),
            "prefixes",
            unit // 4,
            [shape] * near,
            [VMEM] * (len(marked) + len(marked_carries) + near + steps),
            (*marked, *marked_carries, *slots, *carries),
        )
        states.append(exchange(prefix, out_masks))
        marked, marked_carries = marked or slots, marked_carries or carries
    count = near * early
    solved, local, out = call(
        functools.partial(solve_kernel, width, packs, early, max(1, 8 // heads), orders[2]),
        "solve",
        12 * unit,
        [jax.ShapeDtypeStruct((row_count, 2 * columns), jnp.bfloat16), flat, flat],
        [SMEM] + [VMEM] * (4 + near),
        (ridge_weight, ids, queries, key_vectors, value_vectors, *states[0]),
        out_specs=[VMEM, VMEM, HBM],
        scratch_shapes=[
            pltpu.VMEM((max(count, 1), row_count, width), jnp.float32),
            pltpu.SemaphoreType.DMA((max(count, 1),)),
        ],
    )
    for slots in (range(near // 2), range(near // 2, near)):
        out = call(
            functools.partial(readout_kernel, width, heads, early, [orders[3][slot] for slot in slots]),
            "readout",
            2 * unit * len(slots) // near,
            flat,
            [VMEM] * (2 + len(slots)) + [HBM],
            (solved, local, *[states[1][slot] for slot in slots], out),
            out_specs=HBM,
            scratch_shapes=[
                pltpu.VMEM((len(slots), row_count, (heads - early) * width), jnp.float32),
                pltpu.SemaphoreType.DMA((len(slots),)),
            ],
            input_output_aliases={2 + len(slots): 0},
        )
    return out


def solution(mesh):
    outer, inner = mesh.shape["outer"], mesh.shape["inner"]
    finer = Mesh(mesh.devices.reshape(outer, 2, inner // 2), ("outer", "half", "near"))
    tokens = P(("outer", "half", "near"))
    return jax.shard_map(
        on_device, mesh=finer, in_specs=(tokens, tokens, tokens, tokens, P()), out_specs=tokens, check_vma=False
    )
```
